32 devices in a mesh: batch: 8 (over z, y), seq: 4 (over x, core).
Axes of the slice: x: 2, y: 2, z: 4, core: 2. Of those that a mesh axis runs over, the one named last changes fastest.
Arguments:
- tokens: bfloat16 [8, 3072, 512], P('batch', 'seq'), may hold values from -6 to 6
- source: bfloat16 [8, 1536, 512], P('batch', 'seq'), may hold values from -6 to 6
- out_grad: bfloat16 [8, 3072, 512], P('batch', 'seq'), may hold values from -6 to 6
- target_ids: int32 [8, 3072], P('batch', 'seq'), may hold values from 0 to 3, as said below
- source_ids: int32 [8, 1536], P('batch', 'seq'), may hold values from 0 to 3, as said below
- source_len: int32 [8], P('batch'), may hold values from 1488 to 1535
- self_qkv: bfloat16 [512, 1536], replicated, may hold values from -0.25 to 0.25
- self_out: bfloat16 [512, 512], replicated, may hold values from -1 to 1
- cross_q: bfloat16 [512, 512], replicated, may hold values from -0.25 to 0.25
- cross_kv: bfloat16 [512, 1024], replicated, may hold values from -0.25 to 0.25
- cross_out: bfloat16 [512, 512], replicated, may hold values from -1 to 1
- ffn_in: bfloat16 [512, 2048], replicated, may hold values from -0.25 to 0.25
- ffn_out: bfloat16 [2048, 512], replicated, may hold values from -0.125 to 0.125
- norm_gain: float32 [3, 512], replicated, may hold values from 0.25 to 1.75
- norm_bias: float32 [3, 512], replicated, may hold values from -3 to 3
- proj_bias: float32 [4, 512], replicated, may hold values from -3 to 3
- out_bias: float32 [3, 512], replicated, may hold values from -3 to 3
- ffn_bias: float32 [2048], replicated, may hold values from -3 to 3
Outputs:
- output: bfloat16 [8, 3072, 512], P('batch', 'seq')
- tokens_grad: bfloat16 [8, 3072, 512], P('batch', 'seq')
- source_grad: bfloat16 [8, 1536, 512], P('batch', 'seq')
- self_qkv_grad: float32 [512, 1536], replicated
- self_out_grad: float32 [512, 512], replicated
- cross_q_grad: float32 [512, 512], replicated
- cross_kv_grad: float32 [512, 1024], replicated
- cross_out_grad: float32 [512, 512], replicated
- ffn_in_grad: float32 [512, 2048], replicated
- ffn_out_grad: float32 [2048, 512], replicated
- norm_gain_grad: float32 [3, 512], replicated
- norm_bias_grad: float32 [3, 512], replicated
- proj_bias_grad: float32 [4, 512], replicated
- out_bias_grad: float32 [3, 512], replicated
- ffn_bias_grad: float32 [2048], replicated
The draws below stay inside these ranges and needn't reach their ends.
Inputs may be any that keep to these rules, and one draw needn't show every extreme that they name: `target_ids`: along a row the numbers never fall, and each of 0 to 3 occurs. `source_ids`: along a row the numbers never fall, and each of 0 to 3 occurs below the row's source_len.
All inputs are finite; a program needn't handle non-finite values.
Results may differ from the reference program's by a relative error of at most 0.02.
Values may be sent and summed in bfloat16 or wider, within the bound.
No kernel may reach another device: no remote copies, remote signals or barrier semaphores. Data moves between devices by JAX's collectives and lax.ppermute only.
A program may use at most 192 MiB of HBM per device.

```python
import math
import jax
import jax.numpy as jnp
from jax import lax

D = 512
FF = 2048
HEADS = 8
TOK_DEV = 768
PAIRS = 4
SRC_DEV = 384
ROW = 3072
SRC_ROW = 1536
ROWS = 8


def long_pair(key):
    return jax.random.randint(key, (ROWS,), 1, PAIRS - 1)


def pair_numbers(key, lowest, highest, total, longest):
    shorts = jax.random.randint(key, (ROWS, PAIRS), lowest, highest + 1)
    chosen = jnp.arange(PAIRS)[None, :] == longest[:, None]
    others = jnp.sum(jnp.where(chosen, 0, shorts), axis=1)
    lengths = jnp.where(chosen, total - others[:, None], shorts)
    ends = jnp.cumsum(lengths, axis=1)
    places = jnp.arange(total)
    above = places[None, :, None] >= ends[:, None, :PAIRS - 1]
    return jnp.sum(above.astype(jnp.int32), axis=2).astype(jnp.int32)


def draw_target_ids(key, part):
    longest = long_pair(key)
    key = jax.random.fold_in(key, 1)
    return pair_numbers(key, TOK_DEV // 8, TOK_DEV // 4, ROW, longest)


def draw_source_ids(key, part):
    longest = long_pair(key)
    key = jax.random.fold_in(key, 2)
    return pair_numbers(key, SRC_DEV // 4, SRC_DEV // 4 + SRC_DEV // 8, SRC_ROW, longest)


def draw_source_len(key, part):
    key = jax.random.fold_in(key, 3)
    padding = jax.random.randint(key, (ROWS,), 1, SRC_DEV // 8 + 1)
    padding = padding.at[0].set(1).at[ROWS - 1].set(SRC_DEV // 8)
    return (SRC_ROW - padding).astype(jnp.int32)


def shard_levels(key, dims, split, least, top_value):
    def one(position, shards_of):
        steps = jax.random.uniform(jax.random.fold_in(jax.random.fold_in(key, 6), position), (shards_of,), jnp.float32, least / len(split), top_value / len(split))
        return jnp.repeat(jnp.exp(steps), dims[position] // shards_of).reshape((-1,) + (1,) * (len(dims) - position - 1))

    factor_of = one(*split[0])
    for cut in split[1:]:
        factor_of = factor_of * one(*cut)
    return factor_of


def bell_draw(rng, extent, spread, limit, cuts=(), kind=jnp.bfloat16):
    level = shard_levels(rng, extent, cuts, -0.22, 0.18) if cuts else 1.0
    values = jax.random.normal(rng, extent, jnp.float32) * spread * level
    return jnp.minimum(jnp.maximum(values, -limit), limit).astype(kind)


def setup_inputs(seed: int = 0) -> dict:
    key_of = jax.random.split(jax.random.key(seed), 19)
    return {
        "tokens": bell_draw(key_of[0], (ROWS, ROW, D), 1.0, 6.0, ((0, 8), (1, 4))),
        "source": bell_draw(key_of[1], (ROWS, SRC_ROW, D), 1.0, 6.0, ((0, 8), (1, 4))),
        "out_grad": bell_draw(key_of[2], (ROWS, ROW, D), 1.0, 6.0, ((0, 8), (1, 4))),
        "target_ids": draw_target_ids(jax.random.fold_in(key_of[18], 71), 0),
        "source_ids": draw_source_ids(jax.random.fold_in(key_of[18], 71), 0),
        "source_len": draw_source_len(jax.random.fold_in(key_of[18], 71), 0),
        "self_qkv": bell_draw(key_of[6], (D, 3 * D), D ** -0.5, 0.25),
        "self_out": bell_draw(key_of[7], (D, D), (D // 16) ** -0.5, 1.0),
        "cross_q": bell_draw(key_of[8], (D, D), D ** -0.5, 0.25),
        "cross_kv": bell_draw(key_of[9], (D, 2 * D), D ** -0.5, 0.25),
        "cross_out": bell_draw(key_of[10], (D, D), (D // 16) ** -0.5, 1.0),
        "ffn_in": bell_draw(key_of[11], (D, FF), D ** -0.5, 0.25),
        "ffn_out": bell_draw(key_of[12], (FF, D), FF ** -0.5, 0.125),
        "norm_gain": jnp.clip(1.0 + 0.15 * jax.random.normal(key_of[13], (3, D), jnp.float32), 0.25, 1.75),
        "norm_bias": bell_draw(key_of[14], (3, D), 0.3, 3.0, (), jnp.float32),
        "proj_bias": bell_draw(key_of[15], (4, D), 0.3, 3.0, (), jnp.float32),
        "out_bias": bell_draw(key_of[16], (3, D), 0.3, 3.0, (), jnp.float32),
        "ffn_bias": bell_draw(key_of[17], (FF,), 0.3, 3.0, (), jnp.float32),
    }


FINE = lax.Precision.HIGHEST
NEG = -1e+30
EPS = 1e-05

@jax.custom_vjp
def low(v):
    return lax.optimization_barrier(v.astype(jnp.bfloat16)).astype(jnp.float32)

@jax.custom_vjp
def low_back(v):
    return v

def low_keep(v):
    return (low(v), None)

def low_pass(kept, grad):
    return (grad,)

def back_keep(v):
    return (v, None)

def back_low(kept, grad):
    return (low(grad),)
low.defvjp(low_keep, low_pass)
low_back.defvjp(back_keep, back_low)

def matmul(left, right):
    return jnp.dot(left, right, precision=FINE, preferred_element_type=jnp.float32)

def normalize(value, gain, shift):
    centred = value - lax.optimization_barrier(jnp.mean(value, axis=-1, keepdims=True))
    inverse = lax.rsqrt(lax.optimization_barrier(jnp.mean(centred * centred, axis=-1, keepdims=True)) + EPS)
    return centred * inverse * gain + shift

def split_heads(value):
    return value.reshape(value.shape[0], HEADS, D // HEADS)

def attention(queries, keys, values, query_ids, key_ids):
    count = queries.shape[0]
    size = math.gcd(count, 512)
    scale = 1.0 / math.sqrt(D // HEADS)
    query_heads = split_heads(queries).reshape(count // size, size, HEADS, D // HEADS)
    id_blocks = query_ids.reshape(count // size, size)
    key_heads = split_heads(keys)
    value_heads = split_heads(values)

    @jax.checkpoint
    def one_block(pieces):
        block_queries, block_ids = pieces
        scores = low_back(jnp.einsum('qhe,khe->hqk', block_queries, key_heads, precision=FINE) * scale)
        allowed = block_ids[:, None] == key_ids[None, :]
        probs = low(jax.nn.softmax(jnp.where(allowed[None], scores, NEG), axis=-1))
        return jnp.einsum('hqk,khe->qhe', probs, value_heads, precision=FINE)
    mixed = lax.map(one_block, (query_heads, id_blocks))
    return mixed.reshape(count, D)

def row_layer(params, tokens, source, target_ids, source_ids, source_len):
    self_qkv, self_out, cross_q, cross_kv, cross_out, ffn_in, ffn_out, norm_gain, norm_bias, proj_bias, out_bias, ffn_bias = params
    normed_one = low(normalize(tokens, norm_gain[0], norm_bias[0]))
    joined = matmul(normed_one, self_qkv)
    queries = low_back(low(joined[:, :D] + proj_bias[0]))
    keys = low_back(low(joined[:, D:2 * D]))
    values = low_back(low(joined[:, 2 * D:] + proj_bias[1]))
    mixed = low_back(low(attention(queries, keys, values, target_ids, target_ids)))
    branch = low_back(matmul(mixed, self_out) + out_bias[0])
    first = tokens + branch
    normed_two = low(normalize(first, norm_gain[1], norm_bias[1]))
    cross_queries = low_back(low(matmul(normed_two, cross_q) + proj_bias[2]))
    source_joined = matmul(source, cross_kv)
    cross_keys = low_back(low(source_joined[:, :D]))
    cross_values = low_back(low(source_joined[:, D:] + proj_bias[3]))
    places = jnp.arange(source.shape[0]).astype(jnp.int32)
    key_ids = jnp.where(places < source_len.astype(jnp.int32), source_ids, -1).astype(jnp.int32)
    cross_mixed = low_back(low(attention(cross_queries, cross_keys, cross_values, target_ids, key_ids)))
    cross_branch = low_back(matmul(cross_mixed, cross_out) + out_bias[1])
    second = first + cross_branch
    normed_three = low(normalize(second, norm_gain[2], norm_bias[2]))
    hidden = low_back(matmul(normed_three, ffn_in) + ffn_bias)
    active = low(jax.nn.gelu(hidden))
    ffn_branch = low_back(matmul(active, ffn_out) + out_bias[2])
    return second + ffn_branch

def reference(tokens, source, out_grad, target_ids, source_ids, source_len, self_qkv, self_out, cross_q, cross_kv, cross_out, ffn_in, ffn_out, norm_gain, norm_bias, proj_bias, out_bias, ffn_bias):
    weights = tuple((item.astype(jnp.float32) for item in (self_qkv, self_out, cross_q, cross_kv, cross_out, ffn_in, ffn_out, norm_gain, norm_bias, proj_bias, out_bias, ffn_bias)))

    def one_row(totals, pieces):
        token_row, source_row, grad_row, target_row, source_row_ids, length_row = pieces

        def forward(params, token_in, source_in):
            return row_layer(params, token_in, source_in, target_row, source_row_ids, length_row)
        result, pullback = jax.vjp(forward, weights, token_row.astype(jnp.float32), source_row.astype(jnp.float32))
        weight_grads, token_grad, source_grad = pullback(grad_row.astype(jnp.float32))
        totals = jax.tree.map(lambda left, right: left + right, totals, weight_grads)
        return (totals, (result.astype(jnp.bfloat16), token_grad.astype(jnp.bfloat16), source_grad.astype(jnp.bfloat16)))
    zeros = jax.tree.map(jnp.zeros_like, weights)
    totals, stacked = lax.scan(one_row, zeros, (tokens, source, out_grad, target_ids, source_ids, source_len))
    return (stacked[0], stacked[1], stacked[2], totals[0], totals[1], totals[2], totals[3], totals[4], totals[5], totals[6], totals[7], totals[8], totals[9], totals[10], totals[11])
```

```python
import functools
import math

import jax
import jax.numpy as jnp
from jax import lax
from jax.experimental import pallas as pl
from jax.experimental.pallas import tpu as pltpu
from jax.sharding import PartitionSpec as P

HEADS = 8
EPS = 1e-05
F32 = jnp.float32
BF = jnp.bfloat16
LN2 = math.log(2.0)
LOG2E = 1.0 / LN2
VMEM = 60 * 1024 * 1024


def nn(left, right):
    return lax.dot_general(left, right, (((1,), (0,)), ((), ())), preferred_element_type=F32)


def nt(left, right):
    return lax.dot_general(left, right, (((1,), (1,)), ((), ())), preferred_element_type=F32)


def tn(left, right):
    return lax.dot_general(left, right, (((0,), (0,)), ((), ())), preferred_element_type=F32)


def key_marks(ids):
    lane = lax.broadcasted_iota(jnp.int32, (1, 128), 1)
    ids = ids[:, None]
    hit = ((lane < 4) & (lane == ids)) | ((lane == 4) & (ids < 0)) | ((lane >= 5) & (lane <= 9))
    return hit.astype(BF)


def query_marks(ids):
    lane = lax.broadcasted_iota(jnp.int32, (1, 128), 1)
    shut = ((lane < 4) & (lane != ids[:, None])) | (lane == 4)
    return jnp.where(shut, -1e30, 0.0).astype(BF)


def forward_kernel(q_ref, aux_ref, k_ref, v_ref, e_ref, o_ref, aux_out_ref, *, block):
    count = k_ref.shape[0]
    lane = lax.broadcasted_iota(jnp.int32, (1, 128), 1)
    low = lane < 64
    zero = jnp.zeros((), BF)
    one = jnp.ones((), BF)
    q = q_ref[...]
    aux = aux_ref[...]
    done = []
    for head in range(2):
        mine = low if head == 0 else ~low
        query = jnp.concatenate([jnp.where(mine, q, zero), aux], axis=1)
        peak = total = None
        for start in range(0, count, block):
            rows = pl.ds(start, block)
            scores = nt(query, jnp.concatenate([k_ref[rows, :], e_ref[rows, :]], axis=1))
            value = jnp.where(mine, v_ref[rows, :], one)
            largest = jnp.max(scores, axis=1, keepdims=True)
            if peak is None:
                peak = largest
                total = nn(jnp.exp2(scores - peak).astype(BF), value)
            else:
                raised = jnp.maximum(peak, largest)
                total = total * jnp.exp2(peak - raised) + nn(
                    jnp.exp2(scores - raised).astype(BF), value
                )
                peak = raised
        done.append((total, peak))
    top = jnp.where(low, done[0][0], done[1][0])
    below = jnp.where(low, pltpu.roll(done[0][0], 64, 1), pltpu.roll(done[1][0], 64, 1))
    o_ref[...] = (top / below).astype(BF)
    for head in range(2):
        total, peak = done[head]
        weight = total[:, 64:65] if head == 0 else total[:, 0:1]
        minus = -(peak + jnp.log2(weight))
        first = minus.astype(BF)
        rest = minus - first.astype(F32)
        second = rest.astype(BF)
        third = (rest - second.astype(F32)).astype(BF)
        aux_out_ref[head] = jnp.where(
            lane == 5, first, jnp.where(lane == 6, second, jnp.where(lane == 7, third, aux))
        )


def attend(queries, aux, keys, values, marks):
    rows, count = queries.shape[0], keys.shape[0]
    width = queries.shape[1]
    block = 1024 if count % 1024 == 0 else math.gcd(count, 512)
    return pl.pallas_call(
        functools.partial(forward_kernel, block=block),
        grid=(width // 128,),
        in_specs=[
            pl.BlockSpec((rows, 128), lambda i: (0, i)),
            pl.BlockSpec((rows, 128), lambda i: (0, 0)),
            pl.BlockSpec((count, 128), lambda i: (0, i)),
            pl.BlockSpec((count, 128), lambda i: (0, i)),
            pl.BlockSpec((count, 128), lambda i: (0, 0)),
        ],
        out_specs=[
            pl.BlockSpec((rows, 128), lambda i: (0, i)),
            pl.BlockSpec((2, rows, 128), lambda i: (i, 0, 0)),
        ],
        out_shape=[
            jax.ShapeDtypeStruct((rows, width), BF),
            jax.ShapeDtypeStruct((width // 64, rows, 128), BF),
        ],
        compiler_params=pltpu.CompilerParams(vmem_limit_bytes=VMEM),
        name="attend",
    )(queries, aux, keys, values, marks)


def backward_kernel(
    q_ref, do_ref, mix_ref, aux_ref, k_ref, v_ref, e_ref, dq_ref, dk_ref, dv_ref, dq_sum, *, block
):
    count = k_ref.shape[0]
    lane = lax.broadcasted_iota(jnp.int32, (1, 128), 1)
    low = lane < 64
    zero = jnp.zeros((), BF)
    q = q_ref[...]
    do = do_ref[...]
    product = do.astype(F32) * mix_ref[...].astype(F32)
    score_side, probs_side, query_side, grad_side = [], [], [], []
    for head in range(2):
        mine = low if head == 0 else ~low
        q_head = jnp.where(mine, q, zero)
        do_head = jnp.where(mine, do, zero)
        minus = -jnp.sum(jnp.where(mine, product, 0.0), axis=1, keepdims=True)
        first = minus.astype(BF)
        second = (minus - first.astype(F32)).astype(BF)
        extra = jnp.where(lane == 8, first, jnp.where(lane == 9, second, zero))
        score_side.append(jnp.concatenate([q_head, aux_ref[head]], axis=1))
        probs_side.append(jnp.concatenate([do_head, extra], axis=1))
        query_side.append(q_head)
        grad_side.append(do_head)
    for start in range(0, count, block):
        rows = pl.ds(start, block)
        k = k_ref[rows, :]
        e = e_ref[rows, :]
        key = jnp.concatenate([k, e], axis=1)
        value = jnp.concatenate([v_ref[rows, :], e], axis=1)
        dk = dv = None
        for head in range(2):
            mine = low if head == 0 else ~low
            probs = jnp.exp2(nt(key, score_side[head]))
            ds = (probs * nt(value, probs_side[head])).astype(BF)
            dv_head = nn(probs.astype(BF), grad_side[head])
            dk_head = nn(ds, query_side[head])
            dv = dv_head if head == 0 else dv + dv_head
            dk = dk_head if head == 0 else dk + dk_head
            part = tn(jnp.where(mine, k, zero), ds)
            if start == 0 and head == 0:
                dq_sum[...] = part
            else:
                dq_sum[...] += part
        dk_ref[rows, :] = (dk * LN2).astype(BF)
        dv_ref[rows, :] = dv.astype(BF)
    dq_ref[...] = (dq_sum[...].T * 0.125).astype(BF)


def attend_back(queries, grad_mixed, mixed, aux, keys, values, marks):
    rows, count = queries.shape[0], keys.shape[0]
    width = queries.shape[1]
    by_query = pl.BlockSpec((rows, 128), lambda i: (0, i))
    by_key = pl.BlockSpec((count, 128), lambda i: (0, i))
    return pl.pallas_call(
        functools.partial(backward_kernel, block=math.gcd(count, 512)),
        grid=(width // 128,),
        in_specs=[
            by_query,
            by_query,
            by_query,
            pl.BlockSpec((2, rows, 128), lambda i: (i, 0, 0)),
            by_key,
            by_key,
            pl.BlockSpec((count, 128), lambda i: (0, 0)),
        ],
        out_specs=[by_query, by_key, by_key],
        out_shape=[
            jax.ShapeDtypeStruct((rows, width), BF),
            jax.ShapeDtypeStruct((count, width), BF),
            jax.ShapeDtypeStruct((count, width), BF),
        ],
        scratch_shapes=[pltpu.VMEM((128, rows), F32)],
        compiler_params=pltpu.CompilerParams(vmem_limit_bytes=VMEM),
        name="attend_back",
    )(queries, grad_mixed, mixed, aux, keys, values, marks)


def normalize(value, gain, shift):
    centred = value - jnp.mean(value, axis=-1, keepdims=True)
    inverse = lax.rsqrt(jnp.mean(centred * centred, axis=-1, keepdims=True) + EPS)
    unit = centred * inverse
    return (unit * gain + shift, unit, inverse)


def normalize_back(grad_output, unit, inverse, gain):
    scaled = grad_output * gain
    inner = (
        scaled
        - jnp.mean(scaled, axis=-1, keepdims=True)
        - unit * jnp.mean(scaled * unit, axis=-1, keepdims=True)
    )
    return inner * inverse


def swap(value, axis, size, step):
    return lax.ppermute(value, axis, [(i, i ^ step) for i in range(size)])


def gather_row(own, size):
    blocks = [own]
    step = size // 2
    pieces = {0: own}
    while step:
        for place in sorted(pieces):
            pieces[place ^ step] = swap(pieces[place], "seq", size, step)
        step //= 2
    return [pieces[place] for place in range(size)]


def scatter_row(parts, size):
    step = 1
    held = dict(enumerate(parts))
    while step < size:
        kept = {}
        for place in held:
            if not place & step:
                kept[place] = held[place] + swap(held[place | step], "seq", size, step).astype(F32)
        step *= 2
        if step < size:
            held = {
                place: (kept[place].astype(BF) if place & step else kept[place]) for place in kept
            }
        else:
            held = kept
    return held[0]


def sum_all(value, seq, batch):
    steps = [("seq", seq, 1 << k) for k in range(seq.bit_length() - 1)]
    steps += [("batch", batch, 1 << k) for k in range(batch.bit_length() - 1)]
    taken = []
    for axis, size, step in steps:
        rows = value.shape[0]
        if rows % 32:
            value = (value.astype(F32) + swap(value, axis, size, step).astype(F32)).astype(BF)
            continue
        bit = (lax.axis_index(axis) // step) % 2
        half = rows // 2
        kept = lax.dynamic_slice_in_dim(value, bit * half, half, 0)
        sent = lax.dynamic_slice_in_dim(value, (1 - bit) * half, half, 0)
        value = (kept.astype(F32) + swap(sent, axis, size, step).astype(F32)).astype(BF)
        taken.append((axis, size, step, bit))
    for axis, size, step, bit in reversed(taken):
        other = swap(value, axis, size, step)
        first = jnp.where(bit == 0, value, other)
        second = jnp.where(bit == 0, other, value)
        value = jnp.concatenate([first, second], axis=0)
    return value


def body(
    seq,
    batch,
    tokens,
    source,
    out_grad,
    target_ids,
    source_ids,
    source_len,
    self_qkv,
    self_out,
    cross_q,
    cross_kv,
    cross_out,
    ffn_in,
    ffn_out,
    norm_gain,
    norm_bias,
    proj_bias,
    out_bias,
    ffn_bias,
):
    width = tokens.shape[2]
    count = tokens.shape[1]
    scale = LOG2E / math.sqrt(width // HEADS)
    own_ids = target_ids[0]
    places = lax.axis_index("seq") * source.shape[1] + jnp.arange(source.shape[1], dtype=jnp.int32)
    own_source_ids = jnp.where(places < source_len[0], source_ids[0], -1)
    ids = gather_row(jnp.concatenate([own_ids, own_source_ids]), seq)
    token_blocks = gather_row(tokens[0], seq)
    source_blocks = gather_row(source[0], seq)
    marks = key_marks(jnp.concatenate([part[:count] for part in ids]))
    source_marks = key_marks(jnp.concatenate([part[count:] for part in ids]))
    aux = query_marks(own_ids)

    all_tokens = jnp.concatenate(token_blocks, axis=0).astype(F32)
    all_normed, all_unit, all_inverse = normalize(all_tokens, norm_gain[0], norm_bias[0])
    all_normed = all_normed.astype(BF)
    tokens_full = tokens[0].astype(F32)
    own_normed = normalize(tokens_full, norm_gain[0], norm_bias[0])[0].astype(BF)
    queries = ((nn(own_normed, self_qkv[:, :width]) + proj_bias[0]) * scale).astype(BF)
    keys = nn(all_normed, self_qkv[:, width : 2 * width]).astype(BF)
    values = (nn(all_normed, self_qkv[:, 2 * width :]) + proj_bias[1]).astype(BF)
    mixed, self_aux = attend(queries, aux, keys, values, marks)
    first = tokens_full + nn(mixed, self_out) + out_bias[0]
    normed_two, unit_two, inverse_two = normalize(first, norm_gain[1], norm_bias[1])
    normed_two = normed_two.astype(BF)
    cross_queries = ((nn(normed_two, cross_q) + proj_bias[2]) * scale).astype(BF)
    all_source = jnp.concatenate(source_blocks, axis=0)
    cross_keys = nn(all_source, cross_kv[:, :width]).astype(BF)
    cross_values = (nn(all_source, cross_kv[:, width:]) + proj_bias[3]).astype(BF)
    cross_mixed, cross_aux = attend(cross_queries, aux, cross_keys, cross_values, source_marks)
    second = first + nn(cross_mixed, cross_out) + out_bias[1]
    normed_three, unit_three, inverse_three = normalize(second, norm_gain[2], norm_bias[2])
    normed_three = normed_three.astype(BF)
    hidden = nn(normed_three, ffn_in) + ffn_bias
    active, gelu_back = jax.vjp(jax.nn.gelu, hidden)
    active = active.astype(BF)
    output = (second + nn(active, ffn_out) + out_bias[2]).astype(BF)

    grad_low = out_grad[0]
    grad_full = grad_low.astype(F32)
    ffn_out_grad = tn(active, grad_low)
    grad_hidden = gelu_back(nt(grad_low, ffn_out))[0].astype(BF)
    ffn_in_grad = tn(normed_three, grad_hidden)
    ffn_bias_grad = jnp.sum(grad_hidden.astype(F32), axis=0)
    ffn_sum = lax.psum(jnp.concatenate([ffn_in_grad.reshape(-1, width), ffn_out_grad]).astype(BF), ("batch", "seq"))
    grad_three = nt(grad_hidden, ffn_in)
    vectors = {}
    vectors["gain2"] = jnp.sum(grad_three * unit_three, axis=0)
    vectors["shift2"] = jnp.sum(grad_three, axis=0)
    vectors["out2"] = jnp.sum(grad_full, axis=0)
    for k in range(4):
        vectors["ffn%d" % k] = ffn_bias_grad.reshape(4, width)[k]
    grad_second = grad_full + normalize_back(grad_three, unit_three, inverse_three, norm_gain[2])
    second_low = grad_second.astype(BF)
    cross_out_grad = tn(cross_mixed, second_low)
    vectors["out1"] = jnp.sum(second_low.astype(F32), axis=0)
    grad_cross_mixed = nt(second_low, cross_out).astype(BF)
    grad_cross_queries, grad_cross_keys, grad_cross_values = attend_back(
        cross_queries, grad_cross_mixed, cross_mixed, cross_aux, cross_keys, cross_values, source_marks
    )
    cross_q_grad = tn(normed_two, grad_cross_queries)
    vectors["proj2"] = jnp.sum(grad_cross_queries.astype(F32), axis=0)
    vectors["proj3"] = jnp.sum(grad_cross_values.astype(F32), axis=0)
    cross_k_grad = tn(all_source, grad_cross_keys)
    cross_v_grad = tn(all_source, grad_cross_values)
    source_part = (
        nt(grad_cross_keys, cross_kv[:, :width]) + nt(grad_cross_values, cross_kv[:, width:])
    ).astype(BF)
    source_grad = scatter_row(jnp.split(source_part, seq), seq).astype(BF)
    grad_two = nt(grad_cross_queries, cross_q)
    vectors["gain1"] = jnp.sum(grad_two * unit_two, axis=0)
    vectors["shift1"] = jnp.sum(grad_two, axis=0)
    grad_first = grad_second + normalize_back(grad_two, unit_two, inverse_two, norm_gain[1])
    first_low = grad_first.astype(BF)
    self_out_grad = tn(mixed, first_low)
    vectors["out0"] = jnp.sum(first_low.astype(F32), axis=0)
    grad_mixed = nt(first_low, self_out).astype(BF)

    def pack(arrays, names):
        small = jnp.stack([vectors[name] for name in names])
        small = jnp.pad(small, ((0, 128 - len(names)), (0, 0))).T
        return jnp.concatenate([item.astype(BF) for item in arrays] + [small.astype(BF)], axis=1)

    early = ["gain2", "shift2", "out2", "ffn0", "ffn1", "ffn2", "ffn3", "out1", "proj2", "proj3", "gain1", "shift1", "out0"]
    middle = sum_all(pack([cross_out_grad, cross_q_grad, cross_k_grad, cross_v_grad, self_out_grad], early), seq, batch)

    grad_queries, grad_keys, grad_values = attend_back(
        queries, grad_mixed, mixed, self_aux, keys, values, marks
    )
    vectors["proj0"] = jnp.sum(grad_queries.astype(F32), axis=0)
    vectors["proj1"] = jnp.sum(grad_values.astype(F32), axis=0)
    part = nt(grad_keys, self_qkv[:, width : 2 * width]) + nt(grad_values, self_qkv[:, 2 * width :])
    own_part = nt(grad_queries, self_qkv[:, :width])
    blocks = [part[k * count : (k + 1) * count] for k in range(seq)]
    blocks[0] = blocks[0] + own_part
    vectors["gain0"] = sum(
        jnp.sum(blocks[k] * all_unit[k * count : (k + 1) * count], axis=0) for k in range(seq)
    )
    vectors["shift0"] = sum(jnp.sum(blocks[k], axis=0) for k in range(seq))
    grad_one = scatter_row([blocks[k].astype(BF) for k in range(seq)], seq)
    query_grad = tn(own_normed, grad_queries)
    key_grad = tn(all_normed, grad_keys)
    value_grad = tn(all_normed, grad_values)
    late = ["proj0", "proj1", "gain0", "shift0"]
    last = sum_all(pack([query_grad, key_grad, value_grad], late), seq, batch)
    own_unit, own_inverse = all_unit[:count], all_inverse[:count]
    tokens_grad = (
        grad_first + normalize_back(grad_one.astype(F32), own_unit, own_inverse, norm_gain[0])
    ).astype(BF)

    middle = middle.astype(F32)
    last = last.astype(F32)
    ffn_sum = ffn_sum.astype(F32)
    sums = dict(zip(early, middle[:, 5 * width :].T))
    sums.update(zip(late, last[:, 3 * width :].T))
    hidden_rows = ffn_in.shape[0] * ffn_in.shape[1] // width
    return (
        output[None],
        tokens_grad[None],
        source_grad[None],
        last[:, : 3 * width],
        middle[:, 4 * width : 5 * width],
        middle[:, width : 2 * width],
        middle[:, 2 * width : 4 * width],
        middle[:, :width],
        ffn_sum[:hidden_rows].reshape(ffn_in.shape),
        ffn_sum[hidden_rows:],
        jnp.stack([sums["gain0"], sums["gain1"], sums["gain2"]]),
        jnp.stack([sums["shift0"], sums["shift1"], sums["shift2"]]),
        jnp.stack([sums["proj0"], sums["proj1"], sums["proj2"], sums["proj3"]]),
        jnp.stack([sums["out0"], sums["out1"], sums["out2"]]),
        jnp.concatenate([sums["ffn%d" % k] for k in range(4)]),
    )


def solution(mesh):
    row = P("batch", "seq", None)
    flat = P("batch", "seq")
    return jax.shard_map(
        functools.partial(body, mesh.shape["seq"], mesh.shape["batch"]),
        mesh=mesh,
        in_specs=(row, row, row, flat, flat, P("batch")) + (P(),) * 12,
        out_specs=(row, row, row) + (P(),) * 12,
        check_vma=False,
    )
```

```python
import functools
import math

import jax
import jax.numpy as jnp
from jax import lax
from jax.experimental import pallas as pl
from jax.experimental.pallas import tpu as pltpu
from jax.sharding import PartitionSpec as P

HEADS = 8
EPS = 1e-05
F32 = jnp.float32
BF = jnp.bfloat16
LN2 = math.log(2.0)
LOG2E = 1.0 / LN2
VMEM = 60 * 1024 * 1024
SCALE = 1.0 / 8.0
ROOT = math.sqrt(2.0 / math.pi)
CUBE = 0.044715


def nn(left, right):
    return lax.dot_general(left, right, (((1,), (0,)), ((), ())), preferred_element_type=F32)


def nt(left, right):
    return lax.dot_general(left, right, (((1,), (1,)), ((), ())), preferred_element_type=F32)


def tn(left, right):
    return lax.dot_general(left, right, (((0,), (0,)), ((), ())), preferred_element_type=F32)


def shape(rows, columns, kind=BF):
    return jax.ShapeDtypeStruct((rows, columns), kind)


def cost(micros):
    return pl.CostEstimate(flops=int(micros * 3e8), bytes_accessed=0, transcendentals=0)


def run(name, micros, kernel, inputs, outputs, after=(), scalars=(), scratch=()):
    whole = pl.BlockSpec(memory_space=pltpu.VMEM)
    small = pl.BlockSpec(memory_space=pltpu.SMEM)
    away = pl.BlockSpec(memory_space=pl.ANY)

    def wrapped(*refs):
        first = len(scalars) + len(inputs)
        kernel(*refs[:first], *refs[first + len(after) :])

    return pl.pallas_call(
        wrapped,
        in_specs=[small] * len(scalars) + [whole] * len(inputs) + [away] * len(after),
        out_specs=[whole] * len(outputs),
        out_shape=list(outputs),
        scratch_shapes=list(scratch),
        compiler_params=pltpu.CompilerParams(vmem_limit_bytes=VMEM),
        cost_estimate=cost(micros),
        name=name,
    )(*scalars, *inputs, *after)


def key_marks(ids):
    lane = lax.broadcasted_iota(jnp.int32, (128, ids.shape[1]), 0)
    hit = ((lane < 4) & (lane == ids)) | ((lane == 4) & (ids < 0)) | ((lane >= 5) & (lane <= 9))
    return jnp.where(hit, 1.0, 0.0).T.astype(BF)


def query_marks(ids):
    lane = lax.broadcasted_iota(jnp.int32, (128, ids.shape[1]), 0)
    shut = ((lane < 4) & (lane != ids)) | (lane == 4)
    return jnp.where(shut, -1e30, 0.0).T.astype(BF)


def forward_kernel(*refs, blocks, begun, ended):
    q_ref, aux_ref = refs[:2]
    key_refs = refs[2 : 2 + 3 * len(blocks)]
    lane = lax.broadcasted_iota(jnp.int32, (1, 128), 1)
    low = lane < 64
    zero = jnp.zeros((), BF)
    one = jnp.ones((), BF)
    q = q_ref[...]
    aux = aux_ref[...]
    done = []
    for head in range(2):
        mine = low if head == 0 else ~low
        spare = 127 if head == 0 else 63
        query = jnp.concatenate([jnp.where(mine, q, zero), aux], axis=1)
        peak = total = None
        if begun:
            total = refs[2 + 3 * len(blocks)][head]
            peak = jnp.max(jnp.where(lane == spare, total, -jnp.inf), axis=1, keepdims=True)
            total = jnp.where(lane == spare, pltpu.roll(total, 1, 1), total)
        for part, block in enumerate(blocks):
            k_ref, v_ref, e_ref = key_refs[3 * part : 3 * part + 3]
            for start in range(0, k_ref.shape[0], block):
                rows = pl.ds(start, block)
                scores = nt(query, jnp.concatenate([k_ref[rows, :], e_ref[rows, :]], axis=1))
                value = jnp.where(mine, v_ref[rows, :], one)
                largest = jnp.max(scores, axis=1, keepdims=True)
                if peak is None:
                    peak = largest
                    total = nn(jnp.exp2(scores - peak).astype(BF), value)
                else:
                    raised = jnp.maximum(peak, largest)
                    total = total * jnp.exp2(peak - raised) + nn(
                        jnp.exp2(scores - raised).astype(BF), value
                    )
                    peak = raised
        if not ended:
            refs[-1][head] = jnp.where(lane == spare, peak, total)
        done.append((total, peak))
    if not ended:
        return
    o_ref, aux_out_ref = refs[-2:]
    top = jnp.where(low, done[0][0], done[1][0])
    below = jnp.where(low, pltpu.roll(done[0][0], 64, 1), pltpu.roll(done[1][0], 64, 1))
    o_ref[...] = (top / below).astype(BF)
    for head in range(2):
        total, peak = done[head]
        weight = pltpu.roll(total, 64, 1) if head == 0 else total
        minus = -(peak + jnp.log2(jnp.where(low, weight, 1.0)))
        first = minus.astype(BF)
        rest = minus - first.astype(F32)
        second = rest.astype(BF)
        third = (rest - second.astype(F32)).astype(BF)
        aux_out_ref[head] = jnp.where(
            lane == 5, first, jnp.where(lane == 6, second, jnp.where(lane == 7, third, aux))
        )


def largest_block(count, most):
    return max(size for size in range(128, most + 1, 128) if count % size == 0)


def attend(queries, aux, keys, begun=None, ended=True):
    rows, width = queries.shape
    by_head = pl.BlockSpec((2, rows, 128), lambda i: (i, 0, 0))
    specs, flat = [], []
    for k, v, e in keys:
        count = k.shape[0]
        specs += [
            pl.BlockSpec((count, 128), lambda i: (0, i)),
            pl.BlockSpec((count, 128), lambda i: (0, i)),
            pl.BlockSpec((count, 128), lambda i: (0, 0)),
        ]
        flat += [k, v, e]
    if begun is not None:
        specs.append(by_head)
        flat.append(begun)
    blocks = [largest_block(k.shape[0], 1024) for k, v, e in keys]
    totals = jax.ShapeDtypeStruct((width // 64, rows, 128), F32)
    return pl.pallas_call(
        functools.partial(forward_kernel, blocks=blocks, begun=begun is not None, ended=ended),
        grid=(width // 128,),
        in_specs=[
            pl.BlockSpec((rows, 128), lambda i: (0, i)),
            pl.BlockSpec((rows, 128), lambda i: (0, 0)),
        ]
        + specs,
        out_specs=[pl.BlockSpec((rows, 128), lambda i: (0, i)), by_head] if ended else by_head,
        out_shape=[
            jax.ShapeDtypeStruct((rows, width), BF),
            jax.ShapeDtypeStruct((width // 64, rows, 128), BF),
        ]
        if ended
        else totals,
        compiler_params=pltpu.CompilerParams(vmem_limit_bytes=VMEM),
        cost_estimate=cost(26 * sum(k.shape[0] for k, v, e in keys) / 3072),
        name="attend",
    )(queries, aux, *flat)


def backward_kernel(*refs, blocks, fences):
    q_ref, do_ref, mix_ref, aux_ref = refs[:4]
    parts = len(blocks)
    key_refs = refs[4 : 4 + 3 * parts]
    dq_ref, *dkv_refs, dq_sum = refs[4 + 3 * parts + fences :]
    lane = lax.broadcasted_iota(jnp.int32, (1, 128), 1)
    low = lane < 64
    zero = jnp.zeros((), BF)
    q = q_ref[...]
    do = do_ref[...]
    product = do.astype(F32) * mix_ref[...].astype(F32)
    score_side, probs_side, query_side, grad_side = [], [], [], []
    for head in range(2):
        mine = low if head == 0 else ~low
        q_head = jnp.where(mine, q, zero)
        do_head = jnp.where(mine, do, zero)
        minus = -jnp.sum(jnp.where(mine, product, 0.0), axis=1, keepdims=True)
        first = minus.astype(BF)
        second = (minus - first.astype(F32)).astype(BF)
        extra = jnp.where(lane == 8, first, jnp.where(lane == 9, second, zero))
        score_side.append(jnp.concatenate([q_head, aux_ref[head]], axis=1))
        probs_side.append(jnp.concatenate([do_head, extra], axis=1))
        query_side.append(q_head)
        grad_side.append(do_head)
    fresh = True
    for part, block in enumerate(blocks):
        k_ref, v_ref, e_ref = key_refs[3 * part : 3 * part + 3]
        dk_ref, dv_ref = dkv_refs[2 * part : 2 * part + 2]
        for start in range(0, k_ref.shape[0], block):
            rows = pl.ds(start, block)
            k = k_ref[rows, :]
            e = e_ref[rows, :]
            key = jnp.concatenate([k, e], axis=1)
            value = jnp.concatenate([v_ref[rows, :], e], axis=1)
            dk = dv = None
            for head in range(2):
                mine = low if head == 0 else ~low
                probs = jnp.exp2(nt(key, score_side[head]))
                ds = (probs * nt(value, probs_side[head])).astype(BF)
                dv_head = nn(probs.astype(BF), grad_side[head])
                dk_head = nn(ds, query_side[head])
                dv = dv_head if head == 0 else dv + dv_head
                dk = dk_head if head == 0 else dk + dk_head
                piece = tn(jnp.where(mine, k, zero), ds)
                if fresh:
                    dq_sum[...] = piece
                    fresh = False
                else:
                    dq_sum[...] += piece
            dk_ref[rows, :] = (dk * LN2).astype(BF)
            dv_ref[rows, :] = dv.astype(BF)
    dq_ref[...] = (dq_sum[...].T * SCALE).astype(BF)


def attend_back(queries, grad_mixed, mixed, aux, keys, pairs, after=()):
    rows = queries.shape[0]
    base, number = pairs
    by_query = pl.BlockSpec((rows, 128), lambda i: (0, i + base))
    specs, flat, out_specs, out_shapes = [], [], [], []
    for k, v, e in keys:
        count = k.shape[0]
        specs += [
            pl.BlockSpec((count, 128), lambda i: (0, i + base)),
            pl.BlockSpec((count, 128), lambda i: (0, i + base)),
            pl.BlockSpec((count, 128), lambda i: (0, 0)),
        ]
        flat += [k, v, e]
        out_specs += [pl.BlockSpec((count, 128), lambda i: (0, i))] * 2
        out_shapes += [shape(count, 128 * number)] * 2
    return pl.pallas_call(
        functools.partial(
            backward_kernel,
            blocks=[largest_block(k.shape[0], 512) for k, v, e in keys],
            fences=len(after),
        ),
        grid=(number,),
        in_specs=[
            by_query,
            by_query,
            by_query,
            pl.BlockSpec((2, rows, 128), lambda i: (i + base, 0, 0)),
        ]
        + specs
        + [pl.BlockSpec(memory_space=pl.ANY)] * len(after),
        out_specs=[pl.BlockSpec((rows, 128), lambda i: (0, i))] + out_specs,
        out_shape=[shape(rows, 128 * number)] + out_shapes,
        scratch_shapes=[pltpu.VMEM((128, rows), F32)],
        compiler_params=pltpu.CompilerParams(vmem_limit_bytes=VMEM),
        cost_estimate=cost(14 * number * sum(k.shape[0] for k, v, e in keys) / 3072),
        name="attend_back",
    )(queries, grad_mixed, mixed, aux, *flat, *after)


def normalize(value):
    centred = value - jnp.mean(value, axis=-1, keepdims=True)
    inverse = lax.rsqrt(jnp.mean(centred * centred, axis=-1, keepdims=True) + EPS)
    return centred * inverse, inverse


def normalize_back(grad_output, unit, inverse, gain):
    scaled = grad_output * gain
    inner = (
        scaled
        - jnp.mean(scaled, axis=-1, keepdims=True)
        - unit * jnp.mean(scaled * unit, axis=-1, keepdims=True)
    )
    return inner * inverse


def columns_sum(value):
    return jnp.sum(value, axis=0, keepdims=True)


def write_out(total, place, keep_ref, send_ref):
    half = total.shape[0] // 2
    for r, ref in enumerate([keep_ref, send_ref]):
        rows = pl.ds(pl.multiple_of((place[0] ^ r) * half, half), half)
        ref[...] = total[rows, :].astype(BF)


def project_kernel(*refs, count, queries, source):
    token_refs = refs[:count]
    id_refs = refs[count : 2 * count]
    rest = refs[2 * count :]
    if source:
        source_ref, *rest = rest
        rest[8][...] = source_ref[...]
    gain_ref, shift_ref, weight_ref, bias_ref = rest[:4]
    n_ref, k_ref, v_ref, e_ref = rest[4:8]
    rows = token_refs[0].shape[0]
    width = token_refs[0].shape[1]
    for place in range(count):
        unit, _ = normalize(token_refs[place][...].astype(F32))
        normed = (unit * gain_ref[0:1, :] + shift_ref[0:1, :]).astype(BF)
        here = pl.ds(place * rows, rows)
        n_ref[here, :] = normed
        k_ref[here, :] = nn(normed, weight_ref[:, width : 2 * width]).astype(BF)
        v_ref[here, :] = (nn(normed, weight_ref[:, 2 * width :]) + bias_ref[1:2, :]).astype(BF)
        ids = id_refs[place][:, :rows]
        e_ref[here, :] = key_marks(ids)
        if queries and place == 0:
            q_ref, aux_ref = rest[8:10]
            joined = nn(normed, weight_ref[:, :width]) + bias_ref[0:1, :]
            q_ref[...] = (joined * (SCALE * LOG2E)).astype(BF)
            aux_ref[...] = query_marks(ids)


def project(tokens, ids, norm_gain, norm_bias, self_qkv, proj_bias, queries=False, source=(), after=()):
    count = len(tokens)
    rows, width = tokens[0].shape
    inputs = [*tokens, *ids, *source, norm_gain, norm_bias, self_qkv, proj_bias]
    outputs = [shape(count * rows, width)] * 3 + [shape(count * rows, 128)]
    if queries:
        outputs += [shape(rows, width), shape(rows, 128)]
    outputs += [shape(*item.shape) for item in source]
    return run(
        "project",
        6,
        functools.partial(project_kernel, count=count, queries=queries, source=bool(source)),
        inputs,
        outputs,
        after,
    )


def after_self_kernel(mixed, tokens, out, out_bias, gain, shift, cross_q, bias, first_ref, n_ref, q_ref):
    first = tokens[...].astype(F32) + nn(mixed[...], out[...]) + out_bias[0:1, :]
    first_ref[...] = first
    unit, _ = normalize(first)
    normed = (unit * gain[1:2, :] + shift[1:2, :]).astype(BF)
    n_ref[...] = normed
    q_ref[...] = ((nn(normed, cross_q[...]) + bias[2:3, :]) * (SCALE * LOG2E)).astype(BF)


def source_kernel(row_info, *refs, count):
    source_refs = refs[:count]
    id_refs = refs[count : 2 * count]
    weight, bias, k_ref, v_ref, e_ref = refs[2 * count :]
    rows, width = source_refs[0].shape
    for place in range(count):
        here = pl.ds(place * rows, rows)
        joined = nn(source_refs[place][...], weight[...])
        k_ref[here, :] = joined[:, :width].astype(BF)
        v_ref[here, :] = (joined[:, width:] + bias[3:4, :]).astype(BF)
        ids = id_refs[place][:, -rows:]
        spot = (row_info[1] ^ place) * rows + lax.broadcasted_iota(jnp.int32, ids.shape, 1)
        e_ref[here, :] = key_marks(jnp.where(spot < row_info[0], ids, -1))


def ffn_kernel(
    mixed,
    first,
    cross_out,
    out_bias,
    gain,
    shift,
    ffn_in,
    ffn_bias,
    ffn_out,
    out_grad,
    output_ref,
    grad_second_ref,
    grad_mixed_ref,
    grads_ref,
    sums_ref,
    active_ref,
    hidden_ref,
    normed_ref,
    second_ref,
):
    rows = mixed.shape[0]
    tile = rows // 3
    width = mixed.shape[1]
    sums = [0.0] * 4
    bias_sum = 0.0
    for start in range(0, rows, tile):
        here = pl.ds(start, tile)
        second = first[here, :] + nn(mixed[here, :], cross_out[...]) + out_bias[1:2, :]
        unit, inverse = normalize(second)
        normed = (unit * gain[2:3, :] + shift[2:3, :]).astype(BF)
        normed_ref[here, :] = normed
        grad = out_grad[here, :]
        hidden = nn(normed, ffn_in[...]) + ffn_bias[...]
        square = hidden * hidden
        bend = jnp.tanh(ROOT * (hidden + CUBE * (square * hidden)))
        half = 0.5 * (1.0 + bend)
        active = (hidden * half).astype(BF)
        active_ref[here, :] = active
        slope = half + 0.5 * hidden * (1.0 - bend * bend) * (ROOT * (1.0 + 3.0 * CUBE * square))
        grad_hidden32 = nt(grad, ffn_out[...]) * slope
        grad_hidden = grad_hidden32.astype(BF)
        hidden_ref[here, :] = grad_hidden
        bias_sum = bias_sum + columns_sum(grad_hidden.astype(F32))
        output_ref[here, :] = (second + nn(active, ffn_out[...]) + out_bias[2:3, :]).astype(BF)
        grad_three = nt(grad_hidden, ffn_in[...])
        grad32 = grad.astype(F32)
        sums[0] = sums[0] + columns_sum(grad_three * unit)
        sums[1] = sums[1] + columns_sum(grad_three)
        sums[2] = sums[2] + columns_sum(grad32)
        grad_second = grad32 + normalize_back(grad_three, unit, inverse, gain[2:3, :])
        grad_second_ref[here, :] = grad_second
        second_low = grad_second.astype(BF)
        second_ref[here, :] = second_low
        sums[3] = sums[3] + columns_sum(second_low.astype(F32))
        grad_mixed_ref[here, :] = nt(second_low, cross_out[...]).astype(BF)
    units = hidden_ref.shape[1]
    grads_ref[:, :units] = tn(normed_ref[...], hidden_ref[...]).astype(BF)
    for k in range(units // width):
        here = slice(k * width, (k + 1) * width)
        grads_ref[:, units + k * width : units + (k + 1) * width] = tn(
            active_ref[:, here], out_grad[...]
        ).astype(BF)
    grads_ref[:, 2 * units :] = tn(mixed[...], second_ref[...]).astype(BF)
    for k in range(4):
        sums_ref[k : k + 1, :] = sums[k]
        sums_ref[4 + k : 5 + k, :] = bias_sum[:, k * width : (k + 1) * width]


def after_cross_kernel(
    dq_ref,
    cross_q,
    first,
    normed,
    grad_second,
    gain,
    mixed,
    self_out,
    grad_first_ref,
    grad_mixed_ref,
    cross_q_grad,
    self_out_grad,
    sums_ref,
):
    dq = dq_ref[...]
    grad_two = nt(dq, cross_q[...])
    unit, inverse = normalize(first[...])
    grad_first = grad_second[...] + normalize_back(grad_two, unit, inverse, gain[1:2, :])
    grad_first_ref[...] = grad_first
    low = grad_first.astype(BF)
    grad_mixed_ref[...] = nt(low, self_out[...]).astype(BF)
    cross_q_grad[...] = tn(normed[...], dq)
    self_out_grad[...] = tn(mixed[...], low)
    sums_ref[0:1, :] = columns_sum(grad_two * unit)
    sums_ref[1:2, :] = columns_sum(grad_two)
    sums_ref[2:3, :] = columns_sum(low.astype(F32))
    sums_ref[3:4, :] = columns_sum(dq.astype(F32))
    sums_ref[4:8, :] = jnp.zeros((4, dq.shape[1]), F32)


def source_back_kernel(*refs, count):
    places, dk_ref, dv_ref, weight = refs[:4]
    source_refs = refs[4 : 4 + count]
    cross_q_grad, self_out_grad, sums_a, sums_b = refs[4 + count : 8 + count]
    part_refs = refs[8 + count : 8 + 2 * count]
    keep_ref, send_ref, total = refs[8 + 2 * count :]
    rows, width = source_refs[0].shape
    dk = dk_ref[...]
    dv = dv_ref[...]
    pair = jnp.concatenate([dk, dv], axis=1)
    for place in range(count):
        here = slice(place * rows, (place + 1) * rows)
        part_refs[place][...] = nt(pair[here], weight[...]).astype(BF)
    source = jnp.concatenate([ref[...] for ref in source_refs], axis=0)
    total[:, : 2 * width] = tn(source, pair)
    total[:, 2 * width : 3 * width] = self_out_grad[...]
    total[:, 3 * width : 4 * width] = cross_q_grad[...]
    small = jnp.concatenate(
        [
            sums_a[...],
            sums_b[0:4, :],
            columns_sum(dv.astype(F32)),
            jnp.zeros((128 - 13, width), F32),
        ],
        axis=0,
    )
    total[:, 4 * width :] = small.T
    write_out(total, places, keep_ref, send_ref)


def self_post_kernel(*refs, pieces, base, count, spans, begun):
    places = refs[0]
    at = 1
    dq_refs = refs[at : at + pieces]
    at += pieces
    number = len(spans)
    group_refs = []
    for group in range(number):
        group_refs.append((refs[at : at + pieces], refs[at + pieces : at + 2 * pieces]))
        at += 2 * pieces
    normed_refs = refs[at : at + number]
    token_refs = refs[at + number : at + number + count]
    at += number + count
    weight = refs[at]
    at += 1
    if begun:
        earlier = refs[at : at + count]
        small_ref = refs[at + count]
        at += count + 1
    part_refs = refs[at : at + count]
    keep_ref, send_ref = refs[at + count : at + count + 2]
    total = refs[-1]
    rows, width = token_refs[0].shape
    span = 128 * pieces
    weights = [weight[:, k * width + base : k * width + base + span] for k in range(3)]
    weight_pair = jnp.concatenate(weights[1:], axis=1)
    dq = jnp.concatenate([ref[...] for ref in dq_refs], axis=1)
    gain = shift = bias_v = 0.0
    block = 0
    for group, blocks in enumerate(spans):
        dk_refs, dv_refs = group_refs[group]
        for place in range(blocks):
            here = pl.ds(place * rows, rows)
            dk = jnp.concatenate([ref[here, :] for ref in dk_refs], axis=1)
            dv = jnp.concatenate([ref[here, :] for ref in dv_refs], axis=1)
            pair = jnp.concatenate([dk, dv], axis=1)
            grad = nt(pair, weight_pair)
            normed = normed_refs[group][here, :]
            if block == 0:
                grad = grad + nt(dq, weights[0])
                total[:, :span] = tn(normed, dq)
                total[:, span : 3 * span] = tn(normed, pair)
            else:
                total[:, span : 3 * span] += tn(normed, pair)
            if begun:
                grad = grad + earlier[block][...].astype(F32)
                unit, _ = normalize(token_refs[block][...].astype(F32))
                gain = gain + columns_sum(grad * unit)
                shift = shift + columns_sum(grad)
            bias_v = bias_v + columns_sum(dv.astype(F32))
            part_refs[block][...] = grad.astype(BF)
            block += 1
    bias_q = columns_sum(dq.astype(F32))
    if begun:
        bias_q = jnp.concatenate([small_ref[0:1, :], bias_q], axis=1)
        bias_v = jnp.concatenate([small_ref[1:2, :], bias_v], axis=1)
        small = jnp.concatenate([bias_q, bias_v, gain, shift, jnp.zeros((124, width), F32)], axis=0)
        total[:, 3 * span :] = small.T
    else:
        small_out = refs[at + count + 2]
        small_out[0:1, :] = bias_q
        small_out[1:2, :] = bias_v
        small_out[2:8, :] = jnp.zeros((6, span), F32)
    write_out(total, places, keep_ref, send_ref)


def combine_kernel(*refs, plan):
    given = sum(count for kind, count, ways in plan)
    ins, outs = refs[:given], refs[given:]
    i = o = 0
    for kind, count, ways in plan:
        mine = ins[i : i + count]
        i += count
        if kind == "copies":
            total = mine[0][0].astype(F32)
            for place in range(1, ways):
                total = total + mine[0][place].astype(F32)
            total = total.astype(BF)
            for place in range(ways):
                outs[o][place] = total
            o += 1
            continue
        if kind == "beside":
            left = 0
            for first, second in zip(mine[0::2], mine[1::2]):
                columns = first.shape[1]
                outs[o][:, left : left + columns] = (
                    first[...].astype(F32) + second[...].astype(F32)
                ).astype(BF)
                left += columns
            o += 1
            continue
        if kind == "copy":
            outs[o][...] = mine[0][...]
            o += 1
            continue
        size = mine[0].shape[0] // ways
        for way in range(ways):
            here = pl.ds(way * size, size)
            total = mine[0][here, :].astype(F32)
            for ref in mine[1:]:
                total = total + ref[here, :].astype(F32)
            outs[o][...] = total.astype(outs[o].dtype)
            o += 1


def combine(jobs, after=()):
    plan, inputs, outputs, sizes = [], [], [], []
    for job in jobs:
        if job[0] == "copies":
            plan.append(("copies", 1, job[1].shape[0]))
            inputs.append(job[1])
            made = [jax.ShapeDtypeStruct(job[1].shape, BF)]
        elif job[0] == "copy":
            plan.append(("copy", 1, 1))
            inputs.append(job[1])
            made = [jax.ShapeDtypeStruct(job[1].shape, job[1].dtype)]
        elif job[0] == "beside":
            arrays = job[1]
            plan.append(("beside", len(arrays), 1))
            inputs += arrays
            made = [shape(arrays[0].shape[0], sum(item.shape[1] for item in arrays[0::2]))]
        else:
            arrays, ways = job
            rows, columns = arrays[0].shape
            plan.append(("add", len(arrays), ways))
            inputs += arrays
            made = [shape(rows // ways, columns)] * ways
        outputs += made
        sizes.append(len(made))
    flat = run("combine", 2, functools.partial(combine_kernel, plan=plan), inputs, outputs, after)
    results, at = [], 0
    for size in sizes:
        results.append(flat[at : at + size])
        at += size
    return results


def place_kernel(*refs, plan):
    places = refs[0]
    given = sum(parts for parts, cuts in plan)
    ins, outs = refs[1 : 1 + given], refs[1 + given :]
    i = o = 0
    for parts, cuts in plan:
        for group in range(parts):
            ref = ins[i + group]
            block = ref.shape[0]
            number = places[0] ^ group if parts == 2 else 0
            at = 0
            for output, low, columns in cuts:
                first = pl.multiple_of(number * block, block) + low[0]
                outs[o + output][pl.ds(first, block), low[1] : low[1] + columns] = ref[
                    :, at : at + columns
                ].astype(F32)
                at += columns
        i += parts
        o += 1 + max(output for output, low, columns in cuts)


def place(places, parts, after=()):
    plan, inputs, outputs = [], [], []
    for arrays, shapes, cuts in parts:
        plan.append((len(arrays), cuts))
        inputs += arrays
        outputs += [shape(*dims, F32) for dims in shapes]
    return run(
        "place", 5, functools.partial(place_kernel, plan=plan), inputs, outputs, after, [places]
    )


def tokens_kernel(parts_a, parts_b, grad_first, tokens, gain, tokens_grad):
    grad = parts_a[...].astype(F32) + parts_b[...].astype(F32)
    unit, inverse = normalize(tokens[...].astype(F32))
    tokens_grad[...] = (grad_first[...] + normalize_back(grad, unit, inverse, gain[0:1, :])).astype(BF)


def vectors_kernel(small_a, small_b, gains, shifts, projs, outs, ffns):
    first = small_a[...].T
    last = small_b[...].T
    gains[0:1, :] = last[2:3]
    gains[1:2, :] = first[8:9]
    gains[2:3, :] = first[0:1]
    shifts[0:1, :] = last[3:4]
    shifts[1:2, :] = first[9:10]
    shifts[2:3, :] = first[1:2]
    projs[0:2, :] = last[0:2]
    projs[2:3, :] = first[11:12]
    projs[3:4, :] = first[12:13]
    outs[0:1, :] = first[10:11]
    outs[1:2, :] = first[3:4]
    outs[2:3, :] = first[2:3]
    ffns[...] = first[4:8]


def body(
    sizes,
    tokens,
    source,
    out_grad,
    target_ids,
    source_ids,
    source_len,
    self_qkv,
    self_out,
    cross_q,
    cross_kv,
    cross_out,
    ffn_in,
    ffn_out,
    norm_gain,
    norm_bias,
    proj_bias,
    out_bias,
    ffn_bias,
):
    width = tokens.shape[2]
    rows = tokens.shape[1]
    source_rows = source.shape[1]
    row = sizes["side"] * sizes["core"]
    core, side = "core", "side"
    chips = ("batch", "side")
    number = sizes["batch"] * sizes["side"]
    places = lax.axis_index(core).astype(jnp.int32)[None]

    def swap(value, link):
        return lax.ppermute(value, link, [(0, 1), (1, 0)])

    def exchange(half):
        rows, columns = half.shape
        return lax.all_to_all(half.reshape(number, rows // number, columns), chips, 0, 0, tiled=True)

    def regather(copies):
        own = lax.all_to_all(copies, chips, 0, 0, tiled=True)
        return own.reshape(-1, own.shape[2])

    ids = jnp.concatenate([target_ids, source_ids], axis=1)
    by_side = swap(tokens[0], side)
    by_core = swap(tokens[0], core)
    ids_core, ids_side = swap(ids, core), swap(ids, side)
    shared = (norm_gain, norm_bias, self_qkv, proj_bias)
    normed_a, k_a, v_a, e_a, queries, aux = project(
        [tokens[0], by_core], [ids, ids_core], *shared, queries=True
    )
    begun = attend(queries, aux, [(k_a, v_a, e_a)], ended=False)
    (by_side,), (ids_side,) = combine([("copy", by_side), ("copy", ids_side)], [begun])
    token_parts = [tokens[0], by_core, by_side, swap(by_side, core)]
    id_parts = [ids, ids_core, ids_side, swap(ids_side, core)]
    normed_b, k_b, v_b, e_b = project(token_parts[2:3], id_parts[2:3], *shared, after=[begun])
    normed_c, k_c, v_c, e_c, own_source = project(
        token_parts[3:], id_parts[3:], *shared, source=[source[0]], after=[k_b]
    )
    across = lax.ppermute(own_source, (side, core), [(i, row - 1 - i) for i in range(row)])
    source_parts = [own_source, swap(own_source, core), swap(own_source, side), across]
    self_keys = [(k_a, v_a, e_a), (k_b, v_b, e_b), (k_c, v_c, e_c)]
    mixed, self_aux = attend(queries, aux, self_keys[1:], begun)
    normed_parts = [normed_a, normed_b, normed_c]
    position = (lax.axis_index(side) * sizes[core] + lax.axis_index(core)).astype(jnp.int32)
    row_info = jnp.stack([source_len[0], position])
    first, normed_two, cross_queries = run(
        "after_self",
        4,
        after_self_kernel,
        [mixed, tokens[0], self_out, out_bias, norm_gain, norm_bias, cross_q, proj_bias],
        [shape(rows, width, F32), shape(rows, width), shape(rows, width)],
    )
    cross_keys = [
        run(
            "project_source",
        5,
            functools.partial(source_kernel, count=row),
            [*source_parts, *id_parts, cross_kv, proj_bias],
            [shape(row * source_rows, width)] * 2 + [shape(row * source_rows, 128)],
            [mixed],
            [row_info],
        )
    ]
    cross_mixed, cross_aux = attend(cross_queries, aux, cross_keys)

    units = ffn_in.shape[1]
    (
        output,
        grad_second,
        grad_cross_mixed,
        ffn_grads,
        sums_a,
    ) = run(
        "ffn",
        21,
        ffn_kernel,
        [
            cross_mixed,
            first,
            cross_out,
            out_bias,
            norm_gain,
            norm_bias,
            ffn_in,
            ffn_bias[None],
            ffn_out,
            out_grad[0],
        ],
        [
            shape(rows, width),
            shape(rows, width, F32),
            shape(rows, width),
            shape(width, 2 * units + width),
            shape(8, width, F32),
        ],
        scratch=[
            pltpu.VMEM((rows, units), BF),
            pltpu.VMEM((rows, units), BF),
            pltpu.VMEM((rows, width), BF),
            pltpu.VMEM((rows, width), BF),
        ],
    )
    ffn_sums = lax.psum(ffn_grads, ("batch", "side", "core"))
    def backward():
        cross_args = (cross_queries, grad_cross_mixed, cross_mixed, cross_aux, cross_keys)
        dcq, dck, dcv = attend_back(*cross_args, (0, width // 128), [ffn_grads])

        grad_first, grad_mixed, cross_q_grad, self_out_grad, sums_b = run(
            "after_cross",
            6,
            after_cross_kernel,
            [dcq, cross_q, first, normed_two, grad_second, norm_gain, mixed, self_out],
            [
                shape(rows, width, F32),
                shape(rows, width),
                shape(width, width, F32),
                shape(width, width, F32),
                shape(8, width, F32),
            ],
        )
        *source_sums, mid_keep, mid_send = run(
            "source_back",
            9,
            functools.partial(source_back_kernel, count=row),
            [
                dck,
                dcv,
                cross_kv,
                *source_parts,
                cross_q_grad,
                self_out_grad,
                sums_a,
                sums_b,
            ],
            [shape(source_rows, width)] * row
            + [shape(width // 2, 4 * width + 128)] * 2,
            scalars=[places],
            scratch=[pltpu.VMEM((width, 4 * width + 128), F32)],
        )
        mid_come = swap(mid_send, core)
        source_come = [swap(source_sums[1], core), swap(source_sums[3], core)]
        (mid_own,), (source_keep,), (source_send,) = combine(
            [
                ([mid_keep, mid_come], 1),
                ([source_sums[0], source_come[0]], 1),
                ([source_sums[2], source_come[1]], 1),
            ]
        )
        mid_all = exchange(mid_own)
        source_come = swap(source_send, side)

        self_args = (queries, grad_mixed, mixed, self_aux, self_keys)
        back = [attend_back(*self_args, (0, 1), [mid_own])]
        back.append(attend_back(*self_args, (1, 1), [back[0][0]]))
        back.append(attend_back(*self_args, (2, 1), [back[1][0]]))
        (mid_copies,), (source_grad,) = combine(
            [("copies", mid_all), ([source_keep, source_come], 1)], [back[2][0]]
        )
        mid_half = regather(mid_copies)

        def post(pieces, base, earlier, after):
            flat = [item[0] for item in pieces]
            for group in range(len(self_keys)):
                flat += [item[1 + 2 * group] for item in pieces]
                flat += [item[2 + 2 * group] for item in pieces]
            span = 128 * len(pieces)
            wide = 3 * span + (128 if earlier else 0)
            return run(
                "self_post",
                4 * len(pieces),
                functools.partial(
                    self_post_kernel,
                    pieces=len(pieces),
                    base=base,
                    count=row,
                    spans=[item.shape[0] // rows for item in normed_parts],
                    begun=bool(earlier),
                ),
                [*flat, *normed_parts, *token_parts, self_qkv, *earlier],
                [shape(rows, width)] * row
                + [shape(width // 2, wide)] * 2
                + ([] if earlier else [shape(8, span, F32)]),
                after,
                [places],
                [pltpu.VMEM((width, wide), F32)],
            )

        *parts, early_keep, early_send, early_small = post(back[:3], 0, [], [mid_copies])
        early_come = swap(early_send, core)
        back.append(attend_back(*self_args, (3, 1), [early_keep]))
        *parts, late_keep, late_send = post(back[3:], width - 128, [*parts, early_small], [])
        late_come = swap(late_send, core)
        parts_come = [swap(parts[1], core), swap(parts[3], core)]
        (late_own,), (mid_half,) = combine(
            [("beside", [early_keep, early_come, late_keep, late_come]), ("copy", mid_half)]
        )
        (own_sum,), (side_sum,) = combine(
            [([parts[0], parts_come[0]], 1), ([parts[2], parts_come[1]], 1)], [late_own]
        )
        return late_own, own_sum, side_sum, mid_half, source_grad, grad_first

    def nothing():
        return jax.tree.map(lambda item: jnp.zeros(item.shape, item.dtype), jax.eval_shape(backward))

    late_own, own_sum, side_sum, mid_half, source_grad, grad_first = lax.cond(
        source_len[0] > 0, backward, nothing
    )
    late_all = exchange(late_own)
    own_come = swap(side_sum, side)
    mid_halves = [mid_half, swap(mid_half, core)]
    ffn_in_grad, ffn_out_grad, cross_out_grad = place(
        places,
        [
            (
                [ffn_sums],
                [(width, units), (units, width), (width, width)],
                [(0, (0, 0), units)]
                + [(1, (k * width, 0), width) for k in range(units // width)]
                + [(2, (0, 0), width)],
            )
        ],
        [side_sum],
    )
    cross_kv_grad, self_out_grad, cross_q_grad, small_a = place(
        places,
        [
            (
                mid_halves,
                [(width, 2 * width), (width, width), (width, width), (width, 128)],
                [(0, (0, 0), 2 * width), (1, (0, 0), width), (2, (0, 0), width), (3, (0, 0), 128)],
            )
        ],
        [ffn_in_grad],
    )
    (tokens_grad,) = run(
        "tokens",
        4,
        tokens_kernel,
        [own_sum, own_come, grad_first, tokens[0], norm_gain],
        [shape(rows, width)],
        [small_a],
    )
    ((late_copies,),) = combine([("copies", late_all)], [tokens_grad])
    late_half = regather(late_copies)
    late_halves = [late_half, swap(late_half, core)]
    lead = width - 128
    self_qkv_grad, small_b = place(
        places,
        [
            (
                late_halves,
                [(width, 3 * width), (width, 128)],
                [(0, (0, k * width), lead) for k in range(3)]
                + [(0, (0, k * width + lead), 128) for k in range(3)]
                + [(1, (0, 0), 128)],
            )
        ],
    )
    gains, shifts, projs, outs, ffns = run(
        "vectors",
        2,
        vectors_kernel,
        [small_a, small_b],
        [
            shape(3, width, F32),
            shape(3, width, F32),
            shape(4, width, F32),
            shape(3, width, F32),
            shape(4, width, F32),
        ],
    )
    return (
        output[None],
        tokens_grad[None],
        source_grad[None],
        self_qkv_grad,
        self_out_grad,
        cross_q_grad,
        cross_kv_grad,
        cross_out_grad,
        ffn_in_grad,
        ffn_out_grad,
        gains,
        shifts,
        projs,
        outs,
        ffns.reshape(units),
    )


def solution(mesh):
    row_size = mesh.shape["seq"]
    split = jax.sharding.Mesh(
        mesh.devices.reshape(mesh.shape["batch"], row_size // 2, 2), ("batch", "side", "core")
    )
    row = P("batch", ("side", "core"), None)
    flat = P("batch", ("side", "core"))
    return jax.shard_map(
        functools.partial(body, dict(split.shape)),
        mesh=split,
        in_specs=(row, row, row, flat, flat, P("batch")) + (P(),) * 12,
        out_specs=(row, row, row) + (P(),) * 12,
        check_vma=False,
    )
```

```python
import functools
import math

import jax
import jax.numpy as jnp
from jax import lax
from jax.experimental import pallas as pl
from jax.experimental.pallas import tpu as pltpu
from jax.sharding import PartitionSpec as P

HEADS = 8
EPS = 1e-05
F32 = jnp.float32
BF = jnp.bfloat16
LN2 = math.log(2.0)
LOG2E = 1.0 / LN2
VMEM = 60 * 1024 * 1024
SCALE = 1.0 / 8.0
ROOT = math.sqrt(2.0 / math.pi)
CUBE = 0.044715


def nn(left, right):
    return lax.dot_general(left, right, (((1,), (0,)), ((), ())), preferred_element_type=F32)


def nt(left, right):
    return lax.dot_general(left, right, (((1,), (1,)), ((), ())), preferred_element_type=F32)


def tn(left, right):
    return lax.dot_general(left, right, (((0,), (0,)), ((), ())), preferred_element_type=F32)


def shape(rows, columns, kind=BF):
    return jax.ShapeDtypeStruct((rows, columns), kind)


def cost(micros):
    return pl.CostEstimate(flops=int(micros * 3e8), bytes_accessed=0, transcendentals=0)


def run(name, micros, kernel, inputs, outputs, after=(), scalars=(), scratch=()):
    whole = pl.BlockSpec(memory_space=pltpu.VMEM)
    small = pl.BlockSpec(memory_space=pltpu.SMEM)
    away = pl.BlockSpec(memory_space=pl.ANY)

    def wrapped(*refs):
        first = len(scalars) + len(inputs)
        kernel(*refs[:first], *refs[first + len(after) :])

    return pl.pallas_call(
        wrapped,
        in_specs=[small] * len(scalars) + [whole] * len(inputs) + [away] * len(after),
        out_specs=[whole] * len(outputs),
        out_shape=list(outputs),
        scratch_shapes=list(scratch),
        compiler_params=pltpu.CompilerParams(vmem_limit_bytes=VMEM),
        cost_estimate=cost(micros),
        name=name,
    )(*scalars, *inputs, *after)


def key_marks(ids):
    lane = lax.broadcasted_iota(jnp.int32, (128, ids.shape[1]), 0)
    hit = ((lane < 4) & (lane == ids)) | ((lane == 4) & (ids < 0)) | ((lane >= 5) & (lane <= 9))
    return jnp.where(hit, 1.0, 0.0).T.astype(BF)


def query_marks(ids):
    lane = lax.broadcasted_iota(jnp.int32, (128, ids.shape[1]), 0)
    shut = ((lane < 4) & (lane != ids)) | (lane == 4)
    return jnp.where(shut, -1e30, 0.0).T.astype(BF)


def forward_kernel(*refs, blocks, begun, ended):
    q_ref, aux_ref = refs[:2]
    key_refs = refs[2 : 2 + 3 * len(blocks)]
    lane = lax.broadcasted_iota(jnp.int32, (1, 128), 1)
    low = lane < 64
    zero = jnp.zeros((), BF)
    one = jnp.ones((), BF)
    q = q_ref[...]
    aux = aux_ref[...]
    done = []
    for head in range(2):
        mine = low if head == 0 else ~low
        spare = 127 if head == 0 else 63
        query = jnp.concatenate([jnp.where(mine, q, zero), aux], axis=1)
        peak = total = None
        if begun:
            total = refs[2 + 3 * len(blocks)][head]
            peak = jnp.max(jnp.where(lane == spare, total, -jnp.inf), axis=1, keepdims=True)
            total = jnp.where(lane == spare, pltpu.roll(total, 1, 1), total)
        for part, block in enumerate(blocks):
            k_ref, v_ref, e_ref = key_refs[3 * part : 3 * part + 3]
            for start in range(0, k_ref.shape[0], block):
                rows = pl.ds(start, block)
                scores = nt(query, jnp.concatenate([k_ref[rows, :], e_ref[rows, :]], axis=1))
                value = jnp.where(mine, v_ref[rows, :], one)
                largest = jnp.max(scores, axis=1, keepdims=True)
                if peak is None:
                    peak = largest
                    total = nn(jnp.exp2(scores - peak).astype(BF), value)
                else:
                    raised = jnp.maximum(peak, largest)
                    total = total * jnp.exp2(peak - raised) + nn(
                        jnp.exp2(scores - raised).astype(BF), value
                    )
                    peak = raised
        if not ended:
            refs[-1][head] = jnp.where(lane == spare, peak, total)
        done.append((total, peak))
    if not ended:
        return
    o_ref, aux_out_ref = refs[-2:]
    top = jnp.where(low, done[0][0], done[1][0])
    below = jnp.where(low, pltpu.roll(done[0][0], 64, 1), pltpu.roll(done[1][0], 64, 1))
    o_ref[...] = (top / below).astype(BF)
    for head in range(2):
        total, peak = done[head]
        weight = pltpu.roll(total, 64, 1) if head == 0 else total
        minus = -(peak + jnp.log2(jnp.where(low, weight, 1.0)))
        first = minus.astype(BF)
        rest = minus - first.astype(F32)
        second = rest.astype(BF)
        third = (rest - second.astype(F32)).astype(BF)
        aux_out_ref[head] = jnp.where(
            lane == 5, first, jnp.where(lane == 6, second, jnp.where(lane == 7, third, aux))
        )


def largest_block(count, most):
    return max(size for size in range(128, most + 1, 128) if count % size == 0)


def attend(queries, aux, keys, begun=None, ended=True):
    rows, width = queries.shape
    by_head = pl.BlockSpec((2, rows, 128), lambda i: (i, 0, 0))
    specs, flat = [], []
    for k, v, e in keys:
        count = k.shape[0]
        specs += [
            pl.BlockSpec((count, 128), lambda i: (0, i)),
            pl.BlockSpec((count, 128), lambda i: (0, i)),
            pl.BlockSpec((count, 128), lambda i: (0, 0)),
        ]
        flat += [k, v, e]
    if begun is not None:
        specs.append(by_head)
        flat.append(begun)
    blocks = [512 if k.shape[0] % 512 == 0 else largest_block(k.shape[0], 1024) for k, v, e in keys]
    totals = jax.ShapeDtypeStruct((width // 64, rows, 128), F32)
    return pl.pallas_call(
        functools.partial(forward_kernel, blocks=blocks, begun=begun is not None, ended=ended),
        grid=(width // 128,),
        in_specs=[
            pl.BlockSpec((rows, 128), lambda i: (0, i)),
            pl.BlockSpec((rows, 128), lambda i: (0, 0)),
        ]
        + specs,
        out_specs=[pl.BlockSpec((rows, 128), lambda i: (0, i)), by_head] if ended else by_head,
        out_shape=[
            jax.ShapeDtypeStruct((rows, width), BF),
            jax.ShapeDtypeStruct((width // 64, rows, 128), BF),
        ]
        if ended
        else totals,
        compiler_params=pltpu.CompilerParams(vmem_limit_bytes=VMEM),
        cost_estimate=cost(26 * sum(k.shape[0] for k, v, e in keys) / 3072),
        name="attend",
    )(queries, aux, *flat)


def backward_kernel(*refs, blocks, fences):
    q_ref, do_ref, mix_ref, aux_ref = refs[:4]
    parts = len(blocks)
    key_refs = refs[4 : 4 + 3 * parts]
    dq_ref, *dkv_refs, dq_sum = refs[4 + 3 * parts + fences :]
    lane = lax.broadcasted_iota(jnp.int32, (1, 128), 1)
    low = lane < 64
    zero = jnp.zeros((), BF)
    q = q_ref[...]
    do = do_ref[...]
    product = do.astype(F32) * mix_ref[...].astype(F32)
    score_side, probs_side, query_side, grad_side = [], [], [], []
    for head in range(2):
        mine = low if head == 0 else ~low
        q_head = jnp.where(mine, q, zero)
        do_head = jnp.where(mine, do, zero)
        minus = -jnp.sum(jnp.where(mine, product, 0.0), axis=1, keepdims=True)
        first = minus.astype(BF)
        second = (minus - first.astype(F32)).astype(BF)
        extra = jnp.where(lane == 8, first, jnp.where(lane == 9, second, zero))
        score_side.append(jnp.concatenate([q_head, aux_ref[head]], axis=1))
        probs_side.append(jnp.concatenate([do_head, extra], axis=1))
        query_side.append(q_head)
        grad_side.append(do_head)
    fresh = True
    for part, block in enumerate(blocks):
        k_ref, v_ref, e_ref = key_refs[3 * part : 3 * part + 3]
        dk_ref, dv_ref = dkv_refs[2 * part : 2 * part + 2]
        for start in range(0, k_ref.shape[0], block):
            rows = pl.ds(start, block)
            k = k_ref[rows, :]
            e = e_ref[rows, :]
            key = jnp.concatenate([k, e], axis=1)
            value = jnp.concatenate([v_ref[rows, :], e], axis=1)
            dk = dv = None
            for head in range(2):
                mine = low if head == 0 else ~low
                probs = jnp.exp2(nt(key, score_side[head]))
                ds = (probs * nt(value, probs_side[head])).astype(BF)
                dv_head = nn(probs.astype(BF), grad_side[head])
                dk_head = nn(ds, query_side[head])
                dv = dv_head if head == 0 else dv + dv_head
                dk = dk_head if head == 0 else dk + dk_head
                piece = tn(jnp.where(mine, k, zero), ds)
                if fresh:
                    dq_sum[...] = piece
                    fresh = False
                else:
                    dq_sum[...] += piece
            dk_ref[rows, :] = (dk * LN2).astype(BF)
            dv_ref[rows, :] = dv.astype(BF)
    dq_ref[...] = (dq_sum[...].T * SCALE).astype(BF)


def attend_back(queries, grad_mixed, mixed, aux, keys, pairs, after=()):
    rows = queries.shape[0]
    base, number = pairs
    by_query = pl.BlockSpec((rows, 128), lambda i: (0, i + base))
    specs, flat, out_specs, out_shapes = [], [], [], []
    for k, v, e in keys:
        count = k.shape[0]
        specs += [
            pl.BlockSpec((count, 128), lambda i: (0, i + base)),
            pl.BlockSpec((count, 128), lambda i: (0, i + base)),
            pl.BlockSpec((count, 128), lambda i: (0, 0)),
        ]
        flat += [k, v, e]
        out_specs += [pl.BlockSpec((count, 128), lambda i: (0, i))] * 2
        out_shapes += [shape(count, 128 * number)] * 2
    return pl.pallas_call(
        functools.partial(
            backward_kernel,
            blocks=[largest_block(k.shape[0], 768) for k, v, e in keys],
            fences=len(after),
        ),
        grid=(number,),
        in_specs=[
            by_query,
            by_query,
            by_query,
            pl.BlockSpec((2, rows, 128), lambda i: (i + base, 0, 0)),
        ]
        + specs
        + [pl.BlockSpec(memory_space=pl.ANY)] * len(after),
        out_specs=[pl.BlockSpec((rows, 128), lambda i: (0, i))] + out_specs,
        out_shape=[shape(rows, 128 * number)] + out_shapes,
        scratch_shapes=[pltpu.VMEM((128, rows), F32)],
        compiler_params=pltpu.CompilerParams(vmem_limit_bytes=VMEM),
        cost_estimate=cost(14 * number * sum(k.shape[0] for k, v, e in keys) / 3072),
        name="attend_back",
    )(queries, grad_mixed, mixed, aux, *flat, *after)


def normalize(value):
    centred = value - jnp.mean(value, axis=-1, keepdims=True)
    inverse = lax.rsqrt(jnp.mean(centred * centred, axis=-1, keepdims=True) + EPS)
    return centred * inverse, inverse


def normalize_back(grad_output, unit, inverse, gain):
    scaled = grad_output * gain
    inner = (
        scaled
        - jnp.mean(scaled, axis=-1, keepdims=True)
        - unit * jnp.mean(scaled * unit, axis=-1, keepdims=True)
    )
    return inner * inverse


def columns_sum(value):
    return jnp.sum(value, axis=0, keepdims=True)


def write_out(total, place, keep_ref, send_ref):
    half = total.shape[0] // 2
    for r, ref in enumerate([keep_ref, send_ref]):
        rows = pl.ds(pl.multiple_of((place[0] ^ r) * half, half), half)
        ref[...] = total[rows, :].astype(BF)


def project_kernel(*refs, count, queries, source):
    token_refs = refs[:count]
    id_refs = refs[count : 2 * count]
    rest = refs[2 * count :]
    if source:
        source_ref, *rest = rest
        rest[9][...] = source_ref[...]
    gain_ref, shift_ref, weight_ref, bias_ref = rest[:4]
    n_ref, k_ref, v_ref, e_ref, u_ref = rest[4:9]
    rows = token_refs[0].shape[0]
    width = token_refs[0].shape[1]
    for place in range(count):
        unit, _ = normalize(token_refs[place][...].astype(F32))
        normed = (unit * gain_ref[0:1, :] + shift_ref[0:1, :]).astype(BF)
        here = pl.ds(place * rows, rows)
        n_ref[here, :] = normed
        u_ref[here, :] = unit.astype(BF)
        k_ref[here, :] = nn(normed, weight_ref[:, width : 2 * width]).astype(BF)
        v_ref[here, :] = (nn(normed, weight_ref[:, 2 * width :]) + bias_ref[1:2, :]).astype(BF)
        ids = id_refs[place][:, :rows]
        e_ref[here, :] = key_marks(ids)
        if queries and place == 0:
            q_ref, aux_ref = rest[9:11]
            joined = nn(normed, weight_ref[:, :width]) + bias_ref[0:1, :]
            q_ref[...] = (joined * (SCALE * LOG2E)).astype(BF)
            aux_ref[...] = query_marks(ids)


def project(tokens, ids, norm_gain, norm_bias, self_qkv, proj_bias, queries=False, source=(), after=()):
    count = len(tokens)
    rows, width = tokens[0].shape
    inputs = [*tokens, *ids, *source, norm_gain, norm_bias, self_qkv, proj_bias]
    outputs = [shape(count * rows, width)] * 3
    outputs += [shape(count * rows, 128), shape(count * rows, width)]
    if queries:
        outputs += [shape(rows, width), shape(rows, 128)]
    outputs += [shape(*item.shape) for item in source]
    return run(
        "project",
        6,
        functools.partial(project_kernel, count=count, queries=queries, source=bool(source)),
        inputs,
        outputs,
        after,
    )


def after_self_kernel(mixed, tokens, out, out_bias, gain, shift, cross_q, bias, first_ref, n_ref, q_ref):
    first = tokens[...].astype(F32) + nn(mixed[...], out[...]) + out_bias[0:1, :]
    first_ref[...] = first
    unit, _ = normalize(first)
    normed = (unit * gain[1:2, :] + shift[1:2, :]).astype(BF)
    n_ref[...] = normed
    q_ref[...] = ((nn(normed, cross_q[...]) + bias[2:3, :]) * (SCALE * LOG2E)).astype(BF)


def source_kernel(row_info, *refs, count):
    source_refs = refs[:count]
    id_refs = refs[count : 2 * count]
    weight, bias, k_ref, v_ref, e_ref = refs[2 * count :]
    rows, width = source_refs[0].shape
    for place in range(count):
        here = pl.ds(place * rows, rows)
        joined = nn(source_refs[place][...], weight[...])
        k_ref[here, :] = joined[:, :width].astype(BF)
        v_ref[here, :] = (joined[:, width:] + bias[3:4, :]).astype(BF)
        ids = id_refs[place][:, -rows:]
        spot = (row_info[1] ^ place) * rows + lax.broadcasted_iota(jnp.int32, ids.shape, 1)
        e_ref[here, :] = key_marks(jnp.where(spot < row_info[0], ids, -1))


def ffn_kernel(
    mixed,
    first,
    cross_out,
    out_bias,
    gain,
    shift,
    ffn_in,
    ffn_bias,
    ffn_out,
    out_grad,
    output_ref,
    grad_second_ref,
    grad_mixed_ref,
    grads_ref,
    sums_ref,
    active_ref,
    hidden_ref,
    normed_ref,
    second_ref,
):
    rows = mixed.shape[0]
    tile = rows
    width = mixed.shape[1]
    sums = [0.0] * 4
    bias_sum = 0.0
    for start in range(0, rows, tile):
        here = pl.ds(start, tile)
        second = first[here, :] + nn(mixed[here, :], cross_out[...]) + out_bias[1:2, :]
        unit, inverse = normalize(second)
        normed = (unit * gain[2:3, :] + shift[2:3, :]).astype(BF)
        normed_ref[here, :] = normed
        grad = out_grad[here, :]
        hidden = nn(normed, ffn_in[...]) + ffn_bias[...]
        square = hidden * hidden
        bend = jnp.tanh(ROOT * (hidden + CUBE * (square * hidden)))
        half = 0.5 * (1.0 + bend)
        active = (hidden * half).astype(BF)
        active_ref[here, :] = active
        slope = half + 0.5 * hidden * (1.0 - bend * bend) * (ROOT * (1.0 + 3.0 * CUBE * square))
        grad_hidden32 = nt(grad, ffn_out[...]) * slope
        grad_hidden = grad_hidden32.astype(BF)
        hidden_ref[here, :] = grad_hidden
        bias_sum = bias_sum + columns_sum(grad_hidden.astype(F32))
        output_ref[here, :] = (second + nn(active, ffn_out[...]) + out_bias[2:3, :]).astype(BF)
        grad_three = nt(grad_hidden, ffn_in[...])
        grad32 = grad.astype(F32)
        sums[0] = sums[0] + columns_sum(grad_three * unit)
        sums[1] = sums[1] + columns_sum(grad_three)
        sums[2] = sums[2] + columns_sum(grad32)
        grad_second = grad32 + normalize_back(grad_three, unit, inverse, gain[2:3, :])
        grad_second_ref[here, :] = grad_second
        second_low = grad_second.astype(BF)
        second_ref[here, :] = second_low
        sums[3] = sums[3] + columns_sum(second_low.astype(F32))
        grad_mixed_ref[here, :] = nt(second_low, cross_out[...]).astype(BF)
    units = hidden_ref.shape[1]
    grads_ref[:, :units] = tn(normed_ref[...], hidden_ref[...]).astype(BF)
    for k in range(units // width):
        here = slice(k * width, (k + 1) * width)
        grads_ref[:, units + k * width : units + (k + 1) * width] = tn(
            active_ref[:, here], out_grad[...]
        ).astype(BF)
    grads_ref[:, 2 * units :] = tn(mixed[...], second_ref[...]).astype(BF)
    for k in range(4):
        sums_ref[k : k + 1, :] = sums[k]
        sums_ref[4 + k : 5 + k, :] = bias_sum[:, k * width : (k + 1) * width]


def after_cross_kernel(
    dq_ref,
    cross_q,
    first,
    normed,
    grad_second,
    gain,
    mixed,
    self_out,
    grad_first_ref,
    grad_mixed_ref,
    cross_q_grad,
    self_out_grad,
    sums_ref,
):
    dq = dq_ref[...]
    grad_two = nt(dq, cross_q[...])
    unit, inverse = normalize(first[...])
    grad_first = grad_second[...] + normalize_back(grad_two, unit, inverse, gain[1:2, :])
    grad_first_ref[...] = grad_first
    low = grad_first.astype(BF)
    grad_mixed_ref[...] = nt(low, self_out[...]).astype(BF)
    cross_q_grad[...] = tn(normed[...], dq)
    self_out_grad[...] = tn(mixed[...], low)
    sums_ref[0:1, :] = columns_sum(grad_two * unit)
    sums_ref[1:2, :] = columns_sum(grad_two)
    sums_ref[2:3, :] = columns_sum(low.astype(F32))
    sums_ref[3:4, :] = columns_sum(dq.astype(F32))
    sums_ref[4:8, :] = jnp.zeros((4, dq.shape[1]), F32)


def source_back_kernel(*refs, count):
    places, dk_ref, dv_ref, weight = refs[:4]
    source_refs = refs[4 : 4 + count]
    cross_q_grad, self_out_grad, sums_a, sums_b = refs[4 + count : 8 + count]
    part_refs = refs[8 + count : 8 + 2 * count]
    keep_ref, send_ref, total = refs[8 + 2 * count :]
    rows, width = source_refs[0].shape
    dk = dk_ref[...]
    dv = dv_ref[...]
    pair = jnp.concatenate([dk, dv], axis=1)
    for place in range(count):
        here = slice(place * rows, (place + 1) * rows)
        part_refs[place][...] = nt(pair[here], weight[...]).astype(BF)
    source = jnp.concatenate([ref[...] for ref in source_refs], axis=0)
    total[:, : 2 * width] = tn(source, pair)
    total[:, 2 * width : 3 * width] = self_out_grad[...]
    total[:, 3 * width : 4 * width] = cross_q_grad[...]
    small = jnp.concatenate(
        [
            sums_a[...],
            sums_b[0:4, :],
            columns_sum(dv.astype(F32)),
            jnp.zeros((128 - 13, width), F32),
        ],
        axis=0,
    )
    total[:, 4 * width :] = small.T
    write_out(total, places, keep_ref, send_ref)


def self_post_kernel(*refs, pieces, base, count, spans, begun):
    places = refs[0]
    at = 1
    dq_refs = refs[at : at + pieces]
    at += pieces
    number = len(spans)
    group_refs = []
    for group in range(number):
        group_refs.append((refs[at : at + pieces], refs[at + pieces : at + 2 * pieces]))
        at += 2 * pieces
    normed_refs = refs[at : at + number]
    at += number
    weight = refs[at]
    at += 1
    if begun:
        unit_refs = refs[at : at + number]
        at += number
        earlier = refs[at : at + count]
        small_ref = refs[at + count]
        at += count + 1
    part_refs = refs[at : at + count]
    keep_ref, send_ref = refs[at + count : at + count + 2]
    total = refs[-1]
    rows, width = part_refs[0].shape
    span = sum(ref.shape[1] for ref in dq_refs)
    weights = [weight[:, k * width + base : k * width + base + span] for k in range(3)]
    weight_pair = jnp.concatenate(weights[1:], axis=1)
    dq = jnp.concatenate([ref[...] for ref in dq_refs], axis=1)
    gain = shift = bias_v = 0.0
    block = 0
    for group, blocks in enumerate(spans):
        dk_refs, dv_refs = group_refs[group]
        for place in range(blocks):
            here = pl.ds(place * rows, rows)
            dk = jnp.concatenate([ref[here, :] for ref in dk_refs], axis=1)
            dv = jnp.concatenate([ref[here, :] for ref in dv_refs], axis=1)
            pair = jnp.concatenate([dk, dv], axis=1)
            grad = nt(pair, weight_pair)
            normed = normed_refs[group][here, :]
            if block == 0:
                grad = grad + nt(dq, weights[0])
                total[:, :span] = tn(normed, dq)
                total[:, span : 3 * span] = tn(normed, pair)
            else:
                total[:, span : 3 * span] += tn(normed, pair)
            if begun:
                grad = grad + earlier[block][...].astype(F32)
                gain = gain + columns_sum(grad * unit_refs[group][here, :].astype(F32))
                shift = shift + columns_sum(grad)
            bias_v = bias_v + columns_sum(dv.astype(F32))
            part_refs[block][...] = grad.astype(BF)
            block += 1
    bias_q = columns_sum(dq.astype(F32))
    if begun:
        bias_q = jnp.concatenate([small_ref[0:1, :], bias_q], axis=1)
        bias_v = jnp.concatenate([small_ref[1:2, :], bias_v], axis=1)
        small = jnp.concatenate([bias_q, bias_v, gain, shift, jnp.zeros((124, width), F32)], axis=0)
        total[:, 3 * span :] = small.T
    else:
        small_out = refs[at + count + 2]
        small_out[0:1, :] = bias_q
        small_out[1:2, :] = bias_v
        small_out[2:8, :] = jnp.zeros((6, span), F32)
    write_out(total, places, keep_ref, send_ref)


def combine_kernel(*refs, plan):
    given = sum(count for kind, count, ways in plan)
    ins, outs = refs[:given], refs[given:]
    i = o = 0
    for kind, count, ways in plan:
        mine = ins[i : i + count]
        i += count
        if kind == "copies":
            total = mine[0][0].astype(F32)
            for place in range(1, ways):
                total = total + mine[0][place].astype(F32)
            total = total.astype(BF)
            for place in range(ways):
                outs[o][place] = total
            o += 1
            continue
        if kind == "beside":
            left = 0
            for first, second in zip(mine[0::2], mine[1::2]):
                columns = first.shape[1]
                outs[o][:, left : left + columns] = (
                    first[...].astype(F32) + second[...].astype(F32)
                ).astype(BF)
                left += columns
            o += 1
            continue
        if kind == "copy":
            outs[o][...] = mine[0][...]
            o += 1
            continue
        low = 0
        for size in ways:
            here = pl.ds(low, size)
            low += size
            total = mine[0][here, :].astype(F32)
            for ref in mine[1:]:
                total = total + ref[here, :].astype(F32)
            outs[o][...] = total.astype(outs[o].dtype)
            o += 1


def combine(jobs, after=()):
    plan, inputs, outputs, sizes = [], [], [], []
    for job in jobs:
        if job[0] == "copies":
            plan.append(("copies", 1, job[1].shape[0]))
            inputs.append(job[1])
            made = [jax.ShapeDtypeStruct(job[1].shape, BF)]
        elif job[0] == "copy":
            plan.append(("copy", 1, 1))
            inputs.append(job[1])
            made = [jax.ShapeDtypeStruct(job[1].shape, job[1].dtype)]
        elif job[0] == "beside":
            arrays = job[1]
            plan.append(("beside", len(arrays), 1))
            inputs += arrays
            made = [shape(arrays[0].shape[0], sum(item.shape[1] for item in arrays[0::2]))]
        else:
            arrays, ways = job
            rows, columns = arrays[0].shape
            cuts = ways if isinstance(ways, list) else [rows // ways] * ways
            plan.append(("add", len(arrays), cuts))
            inputs += arrays
            made = [shape(size, columns) for size in cuts]
        outputs += made
        sizes.append(len(made))
    flat = run("combine", 2, functools.partial(combine_kernel, plan=plan), inputs, outputs, after)
    results, at = [], 0
    for size in sizes:
        results.append(flat[at : at + size])
        at += size
    return results


def place_kernel(*refs, plan):
    places = refs[0]
    given = sum(parts for parts, cuts in plan)
    ins, outs = refs[1 : 1 + given], refs[1 + given :]
    i = o = 0
    for parts, cuts in plan:
        for group in range(parts):
            ref = ins[i + group]
            block = ref.shape[0]
            number = places[0] ^ group if parts == 2 else 0
            at = 0
            for output, low, columns in cuts:
                first = pl.multiple_of(number * block, block) + low[0]
                outs[o + output][pl.ds(first, block), low[1] : low[1] + columns] = ref[
                    :, at : at + columns
                ].astype(F32)
                at += columns
        i += parts
        o += 1 + max(output for output, low, columns in cuts)


def place(places, parts, after=()):
    plan, inputs, outputs = [], [], []
    for arrays, shapes, cuts in parts:
        plan.append((len(arrays), cuts))
        inputs += arrays
        outputs += [shape(*dims, F32) for dims in shapes]
    return run(
        "place", 5, functools.partial(place_kernel, plan=plan), inputs, outputs, after, [places]
    )


def tokens_kernel(parts, come_a, come_b, grad_first, tokens, gain, tokens_grad):
    come = jnp.concatenate([come_a[...], come_b[...]], axis=0)
    grad = parts[...].astype(F32) + come.astype(F32)
    unit, inverse = normalize(tokens[...].astype(F32))
    tokens_grad[...] = (grad_first[...] + normalize_back(grad, unit, inverse, gain[0:1, :])).astype(BF)


def biases_kernel(small, ffns):
    ffns[...] = small[...].T[4:8]


def finish_kernel(places, half_a, half_b, small_a, qkv, gains, shifts, projs, outs, small_b):
    half, width = half_a.shape[0], small_a.shape[0]
    lead = width - 128
    for group, ref in enumerate([half_a, half_b]):
        rows = pl.ds(pl.multiple_of((places[0] ^ group) * half, half), half)
        for k in range(3):
            qkv[rows, k * width : k * width + lead] = ref[:, k * lead : (k + 1) * lead].astype(F32)
            at = 3 * lead + 128 * k
            qkv[rows, k * width + lead : (k + 1) * width] = ref[:, at : at + 128].astype(F32)
        small_b[rows, :] = ref[:, 3 * width :].astype(F32)
    first = small_a[...].T
    last = small_b[...].T
    gains[0:1, :] = last[2:3]
    gains[1:2, :] = first[8:9]
    gains[2:3, :] = first[0:1]
    shifts[0:1, :] = last[3:4]
    shifts[1:2, :] = first[9:10]
    shifts[2:3, :] = first[1:2]
    projs[0:2, :] = last[0:2]
    projs[2:3, :] = first[11:12]
    projs[3:4, :] = first[12:13]
    outs[0:1, :] = first[10:11]
    outs[1:2, :] = first[3:4]
    outs[2:3, :] = first[2:3]


def body(
    sizes,
    tokens,
    source,
    out_grad,
    target_ids,
    source_ids,
    source_len,
    self_qkv,
    self_out,
    cross_q,
    cross_kv,
    cross_out,
    ffn_in,
    ffn_out,
    norm_gain,
    norm_bias,
    proj_bias,
    out_bias,
    ffn_bias,
):
    width = tokens.shape[2]
    rows = tokens.shape[1]
    source_rows = source.shape[1]
    row = sizes["side"] * sizes["core"]
    core, side = "core", "side"
    chips = ("batch", "side")
    number = sizes["batch"] * sizes["side"]
    places = lax.axis_index(core).astype(jnp.int32)[None]

    def swap(value, link):
        return lax.ppermute(value, link, [(0, 1), (1, 0)])

    def exchange(half):
        rows, columns = half.shape
        return lax.all_to_all(half.reshape(number, rows // number, columns), chips, 0, 0, tiled=True)

    def regather(copies):
        own = lax.all_to_all(copies, chips, 0, 0, tiled=True)
        return own.reshape(-1, own.shape[2])

    ids = jnp.concatenate([target_ids, source_ids], axis=1)
    by_side = swap(tokens[0], side)
    by_core = swap(tokens[0], core)
    ids_core, ids_side = swap(ids, core), swap(ids, side)
    shared = (norm_gain, norm_bias, self_qkv, proj_bias)
    normed_a, k_a, v_a, e_a, unit_a, queries, aux = project(
        [tokens[0], by_core], [ids, ids_core], *shared, queries=True
    )
    begun = attend(queries, aux, [(k_a, v_a, e_a)], ended=False)
    (by_side,), (ids_side,) = combine([("copy", by_side), ("copy", ids_side)], [begun])
    token_parts = [tokens[0], by_core, by_side, swap(by_side, core)]
    id_parts = [ids, ids_core, ids_side, swap(ids_side, core)]
    normed_b, k_b, v_b, e_b, unit_b = project(token_parts[2:3], id_parts[2:3], *shared, after=[begun])
    normed_c, k_c, v_c, e_c, unit_c, own_source = project(
        token_parts[3:], id_parts[3:], *shared, source=[source[0]], after=[k_b]
    )
    across = lax.ppermute(own_source, (side, core), [(i, row - 1 - i) for i in range(row)])
    source_parts = [own_source, swap(own_source, core), swap(own_source, side), across]
    self_keys = [(k_a, v_a, e_a), (k_b, v_b, e_b), (k_c, v_c, e_c)]
    mixed, self_aux = attend(queries, aux, self_keys[1:], begun)
    normed_parts = [normed_a, normed_b, normed_c]
    unit_parts = [unit_a, unit_b, unit_c]
    position = (lax.axis_index(side) * sizes[core] + lax.axis_index(core)).astype(jnp.int32)
    row_info = jnp.stack([source_len[0], position])
    first, normed_two, cross_queries = run(
        "after_self",
        4,
        after_self_kernel,
        [mixed, tokens[0], self_out, out_bias, norm_gain, norm_bias, cross_q, proj_bias],
        [shape(rows, width, F32), shape(rows, width), shape(rows, width)],
    )
    cross_keys = [
        run(
            "project_source",
        5,
            functools.partial(source_kernel, count=row),
            [*source_parts, *id_parts, cross_kv, proj_bias],
            [shape(row * source_rows, width)] * 2 + [shape(row * source_rows, 128)],
            [mixed],
            [row_info],
        )
    ]
    cross_mixed, cross_aux = attend(cross_queries, aux, cross_keys)

    units = ffn_in.shape[1]
    (
        output,
        grad_second,
        grad_cross_mixed,
        ffn_grads,
        sums_a,
    ) = run(
        "ffn",
        21,
        ffn_kernel,
        [
            cross_mixed,
            first,
            cross_out,
            out_bias,
            norm_gain,
            norm_bias,
            ffn_in,
            ffn_bias[None],
            ffn_out,
            out_grad[0],
        ],
        [
            shape(rows, width),
            shape(rows, width, F32),
            shape(rows, width),
            shape(width, 2 * units + width),
            shape(8, width, F32),
        ],
        scratch=[
            pltpu.VMEM((rows, units), BF),
            pltpu.VMEM((rows, units), BF),
            pltpu.VMEM((rows, width), BF),
            pltpu.VMEM((rows, width), BF),
        ],
    )
    ffn_sums = lax.psum(ffn_grads, ("batch", "side", "core"))
    def backward():
        cross_args = (cross_queries, grad_cross_mixed, cross_mixed, cross_aux, cross_keys)
        dcq, dck, dcv = attend_back(*cross_args, (0, width // 128), [ffn_grads])

        grad_first, grad_mixed, cross_q_grad, self_out_grad, sums_b = run(
            "after_cross",
            6,
            after_cross_kernel,
            [dcq, cross_q, first, normed_two, grad_second, norm_gain, mixed, self_out],
            [
                shape(rows, width, F32),
                shape(rows, width),
                shape(width, width, F32),
                shape(width, width, F32),
                shape(8, width, F32),
            ],
        )
        *source_sums, mid_keep, mid_send = run(
            "source_back",
            9,
            functools.partial(source_back_kernel, count=row),
            [
                dck,
                dcv,
                cross_kv,
                *source_parts,
                cross_q_grad,
                self_out_grad,
                sums_a,
                sums_b,
            ],
            [shape(source_rows, width)] * row
            + [shape(width // 2, 4 * width + 128)] * 2,
            scalars=[places],
            scratch=[pltpu.VMEM((width, 4 * width + 128), F32)],
        )
        mid_come = swap(mid_send, core)
        source_come = [swap(source_sums[1], core), swap(source_sums[3], core)]
        self_args = (queries, grad_mixed, mixed, self_aux, self_keys)
        back = [attend_back(*self_args, (0, 1), [mid_keep])]
        (mid_own,), (source_keep,), (source_send,) = combine(
            [
                ([mid_keep, mid_come], 1),
                ([source_sums[0], source_come[0]], 1),
                ([source_sums[2], source_come[1]], 1),
            ],
            [back[0][0]],
        )
        mid_all = exchange(mid_own)
        source_come = swap(source_send, side)
        back.append(attend_back(*self_args, (1, 2), [mid_own]))

        def post(pieces, base, earlier, after):
            flat = [item[0] for item in pieces]
            span = sum(item[0].shape[1] for item in pieces)
            for group in range(len(self_keys)):
                flat += [item[1 + 2 * group] for item in pieces]
                flat += [item[2 + 2 * group] for item in pieces]
            wide = 3 * span + (128 if earlier else 0)
            return run(
                "self_post",
                span // 32,
                functools.partial(
                    self_post_kernel,
                    pieces=len(pieces),
                    base=base,
                    count=row,
                    spans=[item.shape[0] // rows for item in normed_parts],
                    begun=bool(earlier),
                ),
                [*flat, *normed_parts, self_qkv, *earlier],
                [shape(rows, width)] * row
                + [shape(width // 2, wide)] * 2
                + ([] if earlier else [shape(8, span, F32)]),
                after,
                [places],
                [pltpu.VMEM((width, wide), F32)],
            )

        (mid_copies,), (source_grad,) = combine(
            [("copies", mid_all), ([source_keep, source_come], 1)], [back[1][0]]
        )
        mid_half = regather(mid_copies)
        *parts, early_keep, early_send, early_small = post(back, 0, [], [mid_copies])
        early_come = swap(early_send, core)
        last = [attend_back(*self_args, (3, 1), [early_small])]
        *parts, late_keep, late_send = post(
            last, width - 128, [*unit_parts, *parts, early_small], []
        )
        late_come = swap(late_send, core)
        ((late_own,),) = combine([("beside", [early_keep, early_come, late_keep, late_come])])
        return late_own, mid_half, source_grad, grad_first, *parts

    def nothing():
        return jax.tree.map(lambda item: jnp.zeros(item.shape, item.dtype), jax.eval_shape(backward))

    late_own, mid_half, source_grad, grad_first, *parts = lax.cond(
        source_len[0] > 0, backward, nothing
    )
    late_all = exchange(late_own)
    parts_come = [swap(parts[1], core), swap(parts[3], core)]
    mid_halves = [mid_half, swap(mid_half, core)]
    cross_kv_grad, self_out_grad, cross_q_grad, small_a = place(
        places,
        [
            (
                mid_halves,
                [(width, 2 * width), (width, width), (width, width), (width, 128)],
                [(0, (0, 0), 2 * width), (1, (0, 0), width), (2, (0, 0), width), (3, (0, 0), 128)],
            )
        ],
        [late_own],
    )
    cuts = [rows // 4, rows - rows // 4]
    (own_sum,), side_sums = combine(
        [([parts[0], parts_come[0]], 1), ([parts[2], parts_come[1]], cuts)], [small_a]
    )
    own_come = [swap(item, side) for item in side_sums]
    (ffn_biases,) = run("biases", 1, biases_kernel, [small_a], [shape(4, width, F32)], [own_sum])
    ffn_in_grad, ffn_out_grad, cross_out_grad = place(
        places,
        [
            (
                [ffn_sums],
                [(width, units), (units, width), (width, width)],
                [(0, (0, 0), units)]
                + [(1, (k * width, 0), width) for k in range(units // width)]
                + [(2, (0, 0), width)],
            )
        ],
        [ffn_biases],
    )
    ((late_copies,),) = combine([("copies", late_all)], [ffn_in_grad, own_come[0]])
    late_half = regather(late_copies)
    (tokens_grad,) = run(
        "tokens",
        20,
        tokens_kernel,
        [own_sum, *own_come, grad_first, tokens[0], norm_gain],
        [shape(rows, width)],
        [late_copies],
    )
    self_qkv_grad, gains, shifts, projs, outs = run(
        "finish",
        4,
        finish_kernel,
        [late_half, swap(late_half, core), small_a],
        [
            shape(width, 3 * width, F32),
            shape(3, width, F32),
            shape(3, width, F32),
            shape(4, width, F32),
            shape(3, width, F32),
        ],
        [tokens_grad],
        [places],
        [pltpu.VMEM((width, 128), F32)],
    )
    return (
        output[None],
        tokens_grad[None],
        source_grad[None],
        self_qkv_grad,
        self_out_grad,
        cross_q_grad,
        cross_kv_grad,
        cross_out_grad,
        ffn_in_grad,
        ffn_out_grad,
        gains,
        shifts,
        projs,
        outs,
        ffn_biases.reshape(units),
    )


def solution(mesh):
    row_size = mesh.shape["seq"]
    split = jax.sharding.Mesh(
        mesh.devices.reshape(mesh.shape["batch"], row_size // 2, 2), ("batch", "side", "core")
    )
    row = P("batch", ("side", "core"), None)
    flat = P("batch", ("side", "core"))
    return jax.shard_map(
        functools.partial(body, dict(split.shape)),
        mesh=split,
        in_specs=(row, row, row, flat, flat, P("batch")) + (P(),) * 12,
        out_specs=(row, row, row) + (P(),) * 12,
        check_vma=False,
    )
```

```python
import functools
import math

import jax
import jax.numpy as jnp
from jax import lax
from jax.experimental import pallas as pl
from jax.experimental.pallas import tpu as pltpu
from jax.sharding import PartitionSpec as P

HEADS = 8
EPS = 1e-05
F32 = jnp.float32
BF = jnp.bfloat16
LN2 = math.log(2.0)
LOG2E = 1.0 / LN2
VMEM = 60 * 1024 * 1024
SCALE = 1.0 / 8.0
ROOT = math.sqrt(2.0 / math.pi)
CUBE = 0.044715


def nn(left, right):
    return lax.dot_general(left, right, (((1,), (0,)), ((), ())), preferred_element_type=F32)


def nt(left, right):
    return lax.dot_general(left, right, (((1,), (1,)), ((), ())), preferred_element_type=F32)


def tn(left, right):
    return lax.dot_general(left, right, (((0,), (0,)), ((), ())), preferred_element_type=F32)


def shape(rows, columns, kind=BF):
    return jax.ShapeDtypeStruct((rows, columns), kind)


def cost(micros):
    return pl.CostEstimate(flops=int(micros * 3e8), bytes_accessed=0, transcendentals=0)


def run(name, micros, kernel, inputs, outputs, after=(), scalars=(), scratch=()):
    whole = pl.BlockSpec(memory_space=pltpu.VMEM)
    small = pl.BlockSpec(memory_space=pltpu.SMEM)
    away = pl.BlockSpec(memory_space=pl.ANY)

    def wrapped(*refs):
        first = len(scalars) + len(inputs)
        kernel(*refs[:first], *refs[first + len(after) :])

    return pl.pallas_call(
        wrapped,
        in_specs=[small] * len(scalars) + [whole] * len(inputs) + [away] * len(after),
        out_specs=[whole] * len(outputs),
        out_shape=list(outputs),
        scratch_shapes=list(scratch),
        compiler_params=pltpu.CompilerParams(vmem_limit_bytes=VMEM),
        cost_estimate=cost(micros),
        name=name,
    )(*scalars, *inputs, *after)


def key_marks(ids):
    lane = lax.broadcasted_iota(jnp.int32, (128, ids.shape[1]), 0)
    hit = ((lane < 4) & (lane == ids)) | ((lane == 4) & (ids < 0)) | ((lane >= 5) & (lane <= 9))
    return jnp.where(hit, 1.0, 0.0).T.astype(BF)


def query_marks(ids):
    lane = lax.broadcasted_iota(jnp.int32, (128, ids.shape[1]), 0)
    shut = ((lane < 4) & (lane != ids)) | (lane == 4)
    return jnp.where(shut, -1e30, 0.0).T.astype(BF)


def forward_kernel(*refs, blocks, begun, ended):
    q_ref, aux_ref = refs[:2]
    key_refs = refs[2 : 2 + 3 * len(blocks)]
    lane = lax.broadcasted_iota(jnp.int32, (1, 128), 1)
    low = lane < 64
    zero = jnp.zeros((), BF)
    one = jnp.ones((), BF)
    q = q_ref[...]
    aux = aux_ref[...]
    done = []
    for head in range(2):
        mine = low if head == 0 else ~low
        spare = 127 if head == 0 else 63
        query = jnp.concatenate([jnp.where(mine, q, zero), aux], axis=1)
        peak = total = None
        if begun:
            total = refs[2 + 3 * len(blocks)][head]
            peak = jnp.max(jnp.where(lane == spare, total, -jnp.inf), axis=1, keepdims=True)
            total = jnp.where(lane == spare, pltpu.roll(total, 1, 1), total)
        for part, block in enumerate(blocks):
            k_ref, v_ref, e_ref = key_refs[3 * part : 3 * part + 3]
            for start in range(0, k_ref.shape[0], block):
                rows = pl.ds(start, block)
                scores = nt(query, jnp.concatenate([k_ref[rows, :], e_ref[rows, :]], axis=1))
                value = jnp.where(mine, v_ref[rows, :], one)
                largest = jnp.max(scores, axis=1, keepdims=True)
                if peak is None:
                    peak = largest
                    total = nn(jnp.exp2(scores - peak).astype(BF), value)
                else:
                    raised = jnp.maximum(peak, largest)
                    total = total * jnp.exp2(peak - raised) + nn(
                        jnp.exp2(scores - raised).astype(BF), value
                    )
                    peak = raised
        if not ended:
            refs[-1][head] = jnp.where(lane == spare, peak, total)
        done.append((total, peak))
    if not ended:
        return
    o_ref, aux_out_ref = refs[-2:]
    top = jnp.where(low, done[0][0], done[1][0])
    below = jnp.where(low, pltpu.roll(done[0][0], 64, 1), pltpu.roll(done[1][0], 64, 1))
    o_ref[...] = (top / below).astype(BF)
    for head in range(2):
        total, peak = done[head]
        weight = pltpu.roll(total, 64, 1) if head == 0 else total
        minus = -(peak + jnp.log2(jnp.where(low, weight, 1.0)))
        first = minus.astype(BF)
        rest = minus - first.astype(F32)
        second = rest.astype(BF)
        third = (rest - second.astype(F32)).astype(BF)
        aux_out_ref[head] = jnp.where(
            lane == 5, first, jnp.where(lane == 6, second, jnp.where(lane == 7, third, aux))
        )


def largest_block(count, most):
    return max(size for size in range(128, most + 1, 128) if count % size == 0)


def attend(queries, aux, keys, begun=None, ended=True):
    rows, width = queries.shape
    by_head = pl.BlockSpec((2, rows, 128), lambda i: (i, 0, 0))
    specs, flat = [], []
    for k, v, e in keys:
        count = k.shape[0]
        specs += [
            pl.BlockSpec((count, 128), lambda i: (0, i)),
            pl.BlockSpec((count, 128), lambda i: (0, i)),
            pl.BlockSpec((count, 128), lambda i: (0, 0)),
        ]
        flat += [k, v, e]
    if begun is not None:
        specs.append(by_head)
        flat.append(begun)
    blocks = [512 if k.shape[0] % 512 == 0 else largest_block(k.shape[0], 1024) for k, v, e in keys]
    totals = jax.ShapeDtypeStruct((width // 64, rows, 128), F32)
    return pl.pallas_call(
        functools.partial(forward_kernel, blocks=blocks, begun=begun is not None, ended=ended),
        grid=(width // 128,),
        in_specs=[
            pl.BlockSpec((rows, 128), lambda i: (0, i)),
            pl.BlockSpec((rows, 128), lambda i: (0, 0)),
        ]
        + specs,
        out_specs=[pl.BlockSpec((rows, 128), lambda i: (0, i)), by_head] if ended else by_head,
        out_shape=[
            jax.ShapeDtypeStruct((rows, width), BF),
            jax.ShapeDtypeStruct((width // 64, rows, 128), BF),
        ]
        if ended
        else totals,
        compiler_params=pltpu.CompilerParams(vmem_limit_bytes=VMEM),
        cost_estimate=cost(26 * sum(k.shape[0] for k, v, e in keys) / 3072),
        name="attend",
    )(queries, aux, *flat)


def backward_kernel(*refs, blocks, fences):
    q_ref, do_ref, mix_ref, aux_ref = refs[:4]
    parts = len(blocks)
    key_refs = refs[4 : 4 + 3 * parts]
    dq_ref, *dkv_refs, dq_sum = refs[4 + 3 * parts + fences :]
    lane = lax.broadcasted_iota(jnp.int32, (1, 128), 1)
    low = lane < 64
    zero = jnp.zeros((), BF)
    q = q_ref[...]
    do = do_ref[...]
    product = do.astype(F32) * mix_ref[...].astype(F32)
    score_side, probs_side, query_side, grad_side = [], [], [], []
    for head in range(2):
        mine = low if head == 0 else ~low
        q_head = jnp.where(mine, q, zero)
        do_head = jnp.where(mine, do, zero)
        minus = -jnp.sum(jnp.where(mine, product, 0.0), axis=1, keepdims=True)
        first = minus.astype(BF)
        second = (minus - first.astype(F32)).astype(BF)
        extra = jnp.where(lane == 8, first, jnp.where(lane == 9, second, zero))
        score_side.append(jnp.concatenate([q_head, aux_ref[head]], axis=1))
        probs_side.append(jnp.concatenate([do_head, extra], axis=1))
        query_side.append(q_head)
        grad_side.append(do_head)
    fresh = True
    for part, block in enumerate(blocks):
        k_ref, v_ref, e_ref = key_refs[3 * part : 3 * part + 3]
        dk_ref, dv_ref = dkv_refs[2 * part : 2 * part + 2]
        for start in range(0, k_ref.shape[0], block):
            rows = pl.ds(start, block)
            k = k_ref[rows, :]
            e = e_ref[rows, :]
            key = jnp.concatenate([k, e], axis=1)
            value = jnp.concatenate([v_ref[rows, :], e], axis=1)
            dk = dv = None
            for head in range(2):
                mine = low if head == 0 else ~low
                probs = jnp.exp2(nt(key, score_side[head]))
                ds = (probs * nt(value, probs_side[head])).astype(BF)
                dv_head = nn(probs.astype(BF), grad_side[head])
                dk_head = nn(ds, query_side[head])
                dv = dv_head if head == 0 else dv + dv_head
                dk = dk_head if head == 0 else dk + dk_head
                piece = tn(jnp.where(mine, k, zero), ds)
                if fresh:
                    dq_sum[...] = piece
                    fresh = False
                else:
                    dq_sum[...] += piece
            dk_ref[rows, :] = (dk * LN2).astype(BF)
            dv_ref[rows, :] = dv.astype(BF)
    dq_ref[...] = (dq_sum[...].T * SCALE).astype(BF)


def attend_back(queries, grad_mixed, mixed, aux, keys, pairs, after=()):
    rows = queries.shape[0]
    base, number = pairs
    by_query = pl.BlockSpec((rows, 128), lambda i: (0, i + base))
    specs, flat, out_specs, out_shapes = [], [], [], []
    for k, v, e in keys:
        count = k.shape[0]
        specs += [
            pl.BlockSpec((count, 128), lambda i: (0, i + base)),
            pl.BlockSpec((count, 128), lambda i: (0, i + base)),
            pl.BlockSpec((count, 128), lambda i: (0, 0)),
        ]
        flat += [k, v, e]
        out_specs += [pl.BlockSpec((count, 128), lambda i: (0, i))] * 2
        out_shapes += [shape(count, 128 * number)] * 2
    return pl.pallas_call(
        functools.partial(
            backward_kernel,
            blocks=[largest_block(k.shape[0], 768) for k, v, e in keys],
            fences=len(after),
        ),
        grid=(number,),
        in_specs=[
            by_query,
            by_query,
            by_query,
            pl.BlockSpec((2, rows, 128), lambda i: (i + base, 0, 0)),
        ]
        + specs
        + [pl.BlockSpec(memory_space=pl.ANY)] * len(after),
        out_specs=[pl.BlockSpec((rows, 128), lambda i: (0, i))] + out_specs,
        out_shape=[shape(rows, 128 * number)] + out_shapes,
        scratch_shapes=[pltpu.VMEM((128, rows), F32)],
        compiler_params=pltpu.CompilerParams(vmem_limit_bytes=VMEM),
        cost_estimate=cost(14 * number * sum(k.shape[0] for k, v, e in keys) / 3072),
        name="attend_back",
    )(queries, grad_mixed, mixed, aux, *flat, *after)


def normalize(value):
    centred = value - jnp.mean(value, axis=-1, keepdims=True)
    inverse = lax.rsqrt(jnp.mean(centred * centred, axis=-1, keepdims=True) + EPS)
    return centred * inverse, inverse


def normalize_back(grad_output, unit, inverse, gain):
    scaled = grad_output * gain
    inner = (
        scaled
        - jnp.mean(scaled, axis=-1, keepdims=True)
        - unit * jnp.mean(scaled * unit, axis=-1, keepdims=True)
    )
    return inner * inverse


def columns_sum(value):
    return jnp.sum(value, axis=0, keepdims=True)


def write_out(total, place, keep_ref, send_ref):
    half = total.shape[0] // 2
    for r, ref in enumerate([keep_ref, send_ref]):
        rows = pl.ds(pl.multiple_of((place[0] ^ r) * half, half), half)
        ref[...] = total[rows, :].astype(BF)


def project_kernel(*refs, count, queries, source):
    token_refs = refs[:count]
    id_refs = refs[count : 2 * count]
    rest = refs[2 * count :]
    if source:
        source_ref, *rest = rest
        rest[9][...] = source_ref[...]
    gain_ref, shift_ref, weight_ref, bias_ref = rest[:4]
    n_ref, k_ref, v_ref, e_ref, u_ref = rest[4:9]
    rows = token_refs[0].shape[0]
    width = token_refs[0].shape[1]
    for place in range(count):
        unit, _ = normalize(token_refs[place][...].astype(F32))
        normed = (unit * gain_ref[0:1, :] + shift_ref[0:1, :]).astype(BF)
        here = pl.ds(place * rows, rows)
        n_ref[here, :] = normed
        u_ref[here, :] = unit.astype(BF)
        k_ref[here, :] = nn(normed, weight_ref[:, width : 2 * width]).astype(BF)
        v_ref[here, :] = (nn(normed, weight_ref[:, 2 * width :]) + bias_ref[1:2, :]).astype(BF)
        ids = id_refs[place][:, :rows]
        e_ref[here, :] = key_marks(ids)
        if queries and place == 0:
            q_ref, aux_ref = rest[9:11]
            joined = nn(normed, weight_ref[:, :width]) + bias_ref[0:1, :]
            q_ref[...] = (joined * (SCALE * LOG2E)).astype(BF)
            aux_ref[...] = query_marks(ids)


def project(tokens, ids, norm_gain, norm_bias, self_qkv, proj_bias, queries=False, source=(), after=()):
    count = len(tokens)
    rows, width = tokens[0].shape
    inputs = [*tokens, *ids, *source, norm_gain, norm_bias, self_qkv, proj_bias]
    outputs = [shape(count * rows, width)] * 3
    outputs += [shape(count * rows, 128), shape(count * rows, width)]
    if queries:
        outputs += [shape(rows, width), shape(rows, 128)]
    outputs += [shape(*item.shape) for item in source]
    return run(
        "project",
        6,
        functools.partial(project_kernel, count=count, queries=queries, source=bool(source)),
        inputs,
        outputs,
        after,
    )


def after_self_kernel(mixed, tokens, out, out_bias, gain, shift, cross_q, bias, first_ref, n_ref, q_ref):
    first = tokens[...].astype(F32) + nn(mixed[...], out[...]) + out_bias[0:1, :]
    first_ref[...] = first
    unit, _ = normalize(first)
    normed = (unit * gain[1:2, :] + shift[1:2, :]).astype(BF)
    n_ref[...] = normed
    q_ref[...] = ((nn(normed, cross_q[...]) + bias[2:3, :]) * (SCALE * LOG2E)).astype(BF)


def source_kernel(row_info, *refs, count):
    source_refs = refs[:count]
    id_refs = refs[count : 2 * count]
    weight, bias, k_ref, v_ref, e_ref = refs[2 * count :]
    rows, width = source_refs[0].shape
    for place in range(count):
        here = pl.ds(place * rows, rows)
        joined = nn(source_refs[place][...], weight[...])
        k_ref[here, :] = joined[:, :width].astype(BF)
        v_ref[here, :] = (joined[:, width:] + bias[3:4, :]).astype(BF)
        ids = id_refs[place][:, -rows:]
        spot = (row_info[1] ^ place) * rows + lax.broadcasted_iota(jnp.int32, ids.shape, 1)
        e_ref[here, :] = key_marks(jnp.where(spot < row_info[0], ids, -1))


def ffn_kernel(
    mixed,
    first,
    cross_out,
    out_bias,
    gain,
    shift,
    ffn_in,
    ffn_bias,
    ffn_out,
    out_grad,
    output_ref,
    grad_second_ref,
    grad_mixed_ref,
    grads_ref,
    sums_ref,
    active_ref,
    hidden_ref,
    normed_ref,
    second_ref,
):
    rows = mixed.shape[0]
    tile = rows
    width = mixed.shape[1]
    sums = [0.0] * 4
    bias_sum = 0.0
    for start in range(0, rows, tile):
        here = pl.ds(start, tile)
        second = first[here, :] + nn(mixed[here, :], cross_out[...]) + out_bias[1:2, :]
        unit, inverse = normalize(second)
        normed = (unit * gain[2:3, :] + shift[2:3, :]).astype(BF)
        normed_ref[here, :] = normed
        grad = out_grad[here, :]
        hidden = nn(normed, ffn_in[...]) + ffn_bias[...]
        square = hidden * hidden
        bend = jnp.tanh(ROOT * (hidden + CUBE * (square * hidden)))
        half = 0.5 * (1.0 + bend)
        active = (hidden * half).astype(BF)
        active_ref[here, :] = active
        slope = half + 0.5 * hidden * (1.0 - bend * bend) * (ROOT * (1.0 + 3.0 * CUBE * square))
        grad_hidden32 = nt(grad, ffn_out[...]) * slope
        grad_hidden = grad_hidden32.astype(BF)
        hidden_ref[here, :] = grad_hidden
        bias_sum = bias_sum + columns_sum(grad_hidden.astype(F32))
        output_ref[here, :] = (second + nn(active, ffn_out[...]) + out_bias[2:3, :]).astype(BF)
        grad_three = nt(grad_hidden, ffn_in[...])
        grad32 = grad.astype(F32)
        sums[0] = sums[0] + columns_sum(grad_three * unit)
        sums[1] = sums[1] + columns_sum(grad_three)
        sums[2] = sums[2] + columns_sum(grad32)
        grad_second = grad32 + normalize_back(grad_three, unit, inverse, gain[2:3, :])
        grad_second_ref[here, :] = grad_second
        second_low = grad_second.astype(BF)
        second_ref[here, :] = second_low
        sums[3] = sums[3] + columns_sum(second_low.astype(F32))
        grad_mixed_ref[here, :] = nt(second_low, cross_out[...]).astype(BF)
    units = hidden_ref.shape[1]
    grads_ref[:, :units] = tn(normed_ref[...], hidden_ref[...]).astype(BF)
    for k in range(units // width):
        here = slice(k * width, (k + 1) * width)
        grads_ref[:, units + k * width : units + (k + 1) * width] = tn(
            active_ref[:, here], out_grad[...]
        ).astype(BF)
    grads_ref[:, 2 * units :] = tn(mixed[...], second_ref[...]).astype(BF)
    for k in range(4):
        sums_ref[k : k + 1, :] = sums[k]
        sums_ref[4 + k : 5 + k, :] = bias_sum[:, k * width : (k + 1) * width]


def after_cross_kernel(
    dq_ref,
    cross_q,
    first,
    normed,
    grad_second,
    gain,
    mixed,
    self_out,
    grad_first_ref,
    grad_mixed_ref,
    cross_q_grad,
    self_out_grad,
    sums_ref,
):
    dq = dq_ref[...]
    grad_two = nt(dq, cross_q[...])
    unit, inverse = normalize(first[...])
    grad_first = grad_second[...] + normalize_back(grad_two, unit, inverse, gain[1:2, :])
    grad_first_ref[...] = grad_first
    low = grad_first.astype(BF)
    grad_mixed_ref[...] = nt(low, self_out[...]).astype(BF)
    cross_q_grad[...] = tn(normed[...], dq)
    self_out_grad[...] = tn(mixed[...], low)
    sums_ref[0:1, :] = columns_sum(grad_two * unit)
    sums_ref[1:2, :] = columns_sum(grad_two)
    sums_ref[2:3, :] = columns_sum(low.astype(F32))
    sums_ref[3:4, :] = columns_sum(dq.astype(F32))
    sums_ref[4:8, :] = jnp.zeros((4, dq.shape[1]), F32)


def source_back_kernel(*refs, count):
    places, dk_ref, dv_ref, weight = refs[:4]
    source_refs = refs[4 : 4 + count]
    cross_q_grad, self_out_grad, sums_a, sums_b = refs[4 + count : 8 + count]
    part_refs = refs[8 + count : 8 + 2 * count]
    keep_ref, send_ref, total = refs[8 + 2 * count :]
    rows, width = source_refs[0].shape
    dk = dk_ref[...]
    dv = dv_ref[...]
    pair = jnp.concatenate([dk, dv], axis=1)
    for place in range(count):
        here = slice(place * rows, (place + 1) * rows)
        part_refs[place][...] = nt(pair[here], weight[...]).astype(BF)
    source = jnp.concatenate([ref[...] for ref in source_refs], axis=0)
    total[:, : 2 * width] = tn(source, pair)
    total[:, 2 * width : 3 * width] = self_out_grad[...]
    total[:, 3 * width : 4 * width] = cross_q_grad[...]
    small = jnp.concatenate(
        [
            sums_a[...],
            sums_b[0:4, :],
            columns_sum(dv.astype(F32)),
            jnp.zeros((128 - 13, width), F32),
        ],
        axis=0,
    )
    total[:, 4 * width :] = small.T
    write_out(total, places, keep_ref, send_ref)


def self_post_kernel(*refs, pieces, base, count, spans, begun):
    places = refs[0]
    at = 1
    dq_refs = refs[at : at + pieces]
    at += pieces
    number = len(spans)
    group_refs = []
    for group in range(number):
        group_refs.append((refs[at : at + pieces], refs[at + pieces : at + 2 * pieces]))
        at += 2 * pieces
    normed_refs = refs[at : at + number]
    at += number
    weight = refs[at]
    at += 1
    if begun:
        unit_refs = refs[at : at + number]
        at += number
        earlier = refs[at : at + count]
        small_ref = refs[at + count]
        at += count + 1
    part_refs = refs[at : at + count]
    keep_ref, send_ref = refs[at + count : at + count + 2]
    total = refs[-1]
    rows, width = part_refs[0].shape
    span = sum(ref.shape[1] for ref in dq_refs)
    weights = [weight[:, k * width + base : k * width + base + span] for k in range(3)]
    weight_pair = jnp.concatenate(weights[1:], axis=1)
    dq = jnp.concatenate([ref[...] for ref in dq_refs], axis=1)
    gain = shift = bias_v = 0.0
    block = 0
    for group, blocks in enumerate(spans):
        dk_refs, dv_refs = group_refs[group]
        for place in range(blocks):
            here = pl.ds(place * rows, rows)
            dk = jnp.concatenate([ref[here, :] for ref in dk_refs], axis=1)
            dv = jnp.concatenate([ref[here, :] for ref in dv_refs], axis=1)
            pair = jnp.concatenate([dk, dv], axis=1)
            grad = nt(pair, weight_pair)
            normed = normed_refs[group][here, :]
            if block == 0:
                grad = grad + nt(dq, weights[0])
                total[:, :span] = tn(normed, dq)
                total[:, span : 3 * span] = tn(normed, pair)
            else:
                total[:, span : 3 * span] += tn(normed, pair)
            if begun:
                grad = grad + earlier[block][...].astype(F32)
                gain = gain + columns_sum(grad * unit_refs[group][here, :].astype(F32))
                shift = shift + columns_sum(grad)
            bias_v = bias_v + columns_sum(dv.astype(F32))
            part_refs[block][...] = grad.astype(BF)
            block += 1
    bias_q = columns_sum(dq.astype(F32))
    if begun:
        bias_q = jnp.concatenate([small_ref[0:1, :], bias_q], axis=1)
        bias_v = jnp.concatenate([small_ref[1:2, :], bias_v], axis=1)
        small = jnp.concatenate([bias_q, bias_v, gain, shift, jnp.zeros((124, width), F32)], axis=0)
        total[:, 3 * span :] = small.T
    else:
        small_out = refs[at + count + 2]
        small_out[0:1, :] = bias_q
        small_out[1:2, :] = bias_v
        small_out[2:8, :] = jnp.zeros((6, span), F32)
    write_out(total, places, keep_ref, send_ref)


def combine_kernel(*refs, plan):
    given = sum(count for kind, count, ways in plan)
    ins, outs = refs[:given], refs[given:]
    i = o = 0
    for kind, count, ways in plan:
        mine = ins[i : i + count]
        i += count
        if kind == "copies":
            total = mine[0][0].astype(F32)
            for place in range(1, ways):
                total = total + mine[0][place].astype(F32)
            total = total.astype(BF)
            for place in range(ways):
                outs[o][place] = total
            o += 1
            continue
        if kind == "beside":
            left = 0
            for first, second in zip(mine[0::2], mine[1::2]):
                columns = first.shape[1]
                outs[o][:, left : left + columns] = (
                    first[...].astype(F32) + second[...].astype(F32)
                ).astype(BF)
                left += columns
            o += 1
            continue
        if kind == "copy":
            outs[o][...] = mine[0][...]
            o += 1
            continue
        low = 0
        for size in ways:
            here = pl.ds(low, size)
            low += size
            total = mine[0][here, :].astype(F32)
            for ref in mine[1:]:
                total = total + ref[here, :].astype(F32)
            outs[o][...] = total.astype(outs[o].dtype)
            o += 1


def combine(jobs, after=()):
    plan, inputs, outputs, sizes = [], [], [], []
    for job in jobs:
        if job[0] == "copies":
            plan.append(("copies", 1, job[1].shape[0]))
            inputs.append(job[1])
            made = [jax.ShapeDtypeStruct(job[1].shape, BF)]
        elif job[0] == "copy":
            plan.append(("copy", 1, 1))
            inputs.append(job[1])
            made = [jax.ShapeDtypeStruct(job[1].shape, job[1].dtype)]
        elif job[0] == "beside":
            arrays = job[1]
            plan.append(("beside", len(arrays), 1))
            inputs += arrays
            made = [shape(arrays[0].shape[0], sum(item.shape[1] for item in arrays[0::2]))]
        else:
            arrays, ways = job
            rows, columns = arrays[0].shape
            cuts = ways if isinstance(ways, list) else [rows // ways] * ways
            plan.append(("add", len(arrays), cuts))
            inputs += arrays
            made = [shape(size, columns) for size in cuts]
        outputs += made
        sizes.append(len(made))
    flat = run("combine", 2, functools.partial(combine_kernel, plan=plan), inputs, outputs, after)
    results, at = [], 0
    for size in sizes:
        results.append(flat[at : at + size])
        at += size
    return results


def place_kernel(*refs, plan):
    places = refs[0]
    given = sum(parts for parts, cuts in plan)
    ins, outs = refs[1 : 1 + given], refs[1 + given :]
    i = o = 0
    for parts, cuts in plan:
        for group in range(parts):
            ref = ins[i + group]
            block = ref.shape[0]
            number = places[0] ^ group if parts == 2 else 0
            at = 0
            for output, low, columns in cuts:
                first = pl.multiple_of(number * block, block) + low[0]
                outs[o + output][pl.ds(first, block), low[1] : low[1] + columns] = ref[
                    :, at : at + columns
                ].astype(F32)
                at += columns
        i += parts
        o += 1 + max(output for output, low, columns in cuts)


def place(places, parts, after=()):
    plan, inputs, outputs = [], [], []
    for arrays, shapes, cuts in parts:
        plan.append((len(arrays), cuts))
        inputs += arrays
        outputs += [shape(*dims, F32) for dims in shapes]
    return run(
        "place", 5, functools.partial(place_kernel, plan=plan), inputs, outputs, after, [places]
    )


def tokens_kernel(parts, come_a, come_b, grad_first, tokens, gain, tokens_grad):
    come = jnp.concatenate([come_a[...], come_b[...]], axis=0)
    grad = parts[...].astype(F32) + come.astype(F32)
    unit, inverse = normalize(tokens[...].astype(F32))
    tokens_grad[...] = (grad_first[...] + normalize_back(grad, unit, inverse, gain[0:1, :])).astype(BF)


def biases_kernel(small, ffns):
    ffns[...] = small[...].T[4:8]


def finish_kernel(places, half_a, half_b, small_a, qkv, gains, shifts, projs, outs, small_b):
    half, width = half_a.shape[0], small_a.shape[0]
    lead = width - 128
    for group, ref in enumerate([half_a, half_b]):
        rows = pl.ds(pl.multiple_of((places[0] ^ group) * half, half), half)
        for k in range(3):
            qkv[rows, k * width : k * width + lead] = ref[:, k * lead : (k + 1) * lead].astype(F32)
            at = 3 * lead + 128 * k
            qkv[rows, k * width + lead : (k + 1) * width] = ref[:, at : at + 128].astype(F32)
        small_b[rows, :] = ref[:, 3 * width :].astype(F32)
    first = small_a[...].T
    last = small_b[...].T
    gains[0:1, :] = last[2:3]
    gains[1:2, :] = first[8:9]
    gains[2:3, :] = first[0:1]
    shifts[0:1, :] = last[3:4]
    shifts[1:2, :] = first[9:10]
    shifts[2:3, :] = first[1:2]
    projs[0:2, :] = last[0:2]
    projs[2:3, :] = first[11:12]
    projs[3:4, :] = first[12:13]
    outs[0:1, :] = first[10:11]
    outs[1:2, :] = first[3:4]
    outs[2:3, :] = first[2:3]


def body(
    sizes,
    tokens,
    source,
    out_grad,
    target_ids,
    source_ids,
    source_len,
    self_qkv,
    self_out,
    cross_q,
    cross_kv,
    cross_out,
    ffn_in,
    ffn_out,
    norm_gain,
    norm_bias,
    proj_bias,
    out_bias,
    ffn_bias,
):
    width = tokens.shape[2]
    rows = tokens.shape[1]
    source_rows = source.shape[1]
    row = sizes["side"] * sizes["core"]
    core, side = "core", "side"
    chips = ("batch", "side")
    number = sizes["batch"] * sizes["side"]
    places = lax.axis_index(core).astype(jnp.int32)[None]

    def swap(value, link):
        return lax.ppermute(value, link, [(0, 1), (1, 0)])

    def exchange(half):
        rows, columns = half.shape
        return lax.all_to_all(half.reshape(number, rows // number, columns), chips, 0, 0, tiled=True)

    def regather(copies):
        own = lax.all_to_all(copies, chips, 0, 0, tiled=True)
        return own.reshape(-1, own.shape[2])

    ids = jnp.concatenate([target_ids, source_ids], axis=1)
    by_side = swap(tokens[0], side)
    by_core = swap(tokens[0], core)
    ids_core, ids_side = swap(ids, core), swap(ids, side)
    shared = (norm_gain, norm_bias, self_qkv, proj_bias)
    normed_a, k_a, v_a, e_a, unit_a, queries, aux = project(
        [tokens[0], by_core], [ids, ids_core], *shared, queries=True
    )
    begun = attend(queries, aux, [(k_a, v_a, e_a)], ended=False)
    (by_side,), (ids_side,) = combine([("copy", by_side), ("copy", ids_side)], [begun])
    token_parts = [tokens[0], by_core, by_side, swap(by_side, core)]
    id_parts = [ids, ids_core, ids_side, swap(ids_side, core)]
    normed_b, k_b, v_b, e_b, unit_b = project(token_parts[2:3], id_parts[2:3], *shared, after=[begun])
    normed_c, k_c, v_c, e_c, unit_c, own_source = project(
        token_parts[3:], id_parts[3:], *shared, source=[source[0]], after=[k_b]
    )
    across = lax.ppermute(own_source, (side, core), [(i, row - 1 - i) for i in range(row)])
    source_parts = [own_source, swap(own_source, core), swap(own_source, side), across]
    self_keys = [(k_a, v_a, e_a), (k_b, v_b, e_b), (k_c, v_c, e_c)]
    mixed, self_aux = attend(queries, aux, self_keys[1:], begun)
    normed_parts = [normed_a, normed_b, normed_c]
    unit_parts = [unit_a, unit_b, unit_c]
    position = (lax.axis_index(side) * sizes[core] + lax.axis_index(core)).astype(jnp.int32)
    row_info = jnp.stack([source_len[0], position])
    first, normed_two, cross_queries = run(
        "after_self",
        4,
        after_self_kernel,
        [mixed, tokens[0], self_out, out_bias, norm_gain, norm_bias, cross_q, proj_bias],
        [shape(rows, width, F32), shape(rows, width), shape(rows, width)],
    )
    cross_keys = [
        run(
            "project_source",
        5,
            functools.partial(source_kernel, count=row),
            [*source_parts, *id_parts, cross_kv, proj_bias],
            [shape(row * source_rows, width)] * 2 + [shape(row * source_rows, 128)],
            [mixed],
            [row_info],
        )
    ]
    cross_mixed, cross_aux = attend(cross_queries, aux, cross_keys)

    units = ffn_in.shape[1]
    (
        output,
        grad_second,
        grad_cross_mixed,
        ffn_grads,
        sums_a,
    ) = run(
        "ffn",
        21,
        ffn_kernel,
        [
            cross_mixed,
            first,
            cross_out,
            out_bias,
            norm_gain,
            norm_bias,
            ffn_in,
            ffn_bias[None],
            ffn_out,
            out_grad[0],
        ],
        [
            shape(rows, width),
            shape(rows, width, F32),
            shape(rows, width),
            shape(width, 2 * units + width),
            shape(8, width, F32),
        ],
        scratch=[
            pltpu.VMEM((rows, units), BF),
            pltpu.VMEM((rows, units), BF),
            pltpu.VMEM((rows, width), BF),
            pltpu.VMEM((rows, width), BF),
        ],
    )
    ffn_sums = lax.psum(ffn_grads, ("batch", "side", "core"))
    def backward():
        cross_args = (cross_queries, grad_cross_mixed, cross_mixed, cross_aux, cross_keys)
        dcq, dck, dcv = attend_back(*cross_args, (0, width // 128), [ffn_grads])

        grad_first, grad_mixed, cross_q_grad, self_out_grad, sums_b = run(
            "after_cross",
            6,
            after_cross_kernel,
            [dcq, cross_q, first, normed_two, grad_second, norm_gain, mixed, self_out],
            [
                shape(rows, width, F32),
                shape(rows, width),
                shape(width, width, F32),
                shape(width, width, F32),
                shape(8, width, F32),
            ],
        )
        *source_sums, mid_keep, mid_send = run(
            "source_back",
            9,
            functools.partial(source_back_kernel, count=row),
            [
                dck,
                dcv,
                cross_kv,
                *source_parts,
                cross_q_grad,
                self_out_grad,
                sums_a,
                sums_b,
            ],
            [shape(source_rows, width)] * row
            + [shape(width // 2, 4 * width + 128)] * 2,
            scalars=[places],
            scratch=[pltpu.VMEM((width, 4 * width + 128), F32)],
        )
        mid_come = swap(mid_send, core)
        source_come = [swap(source_sums[1], core), swap(source_sums[3], core)]
        self_args = (queries, grad_mixed, mixed, self_aux, self_keys)
        back = [attend_back(*self_args, (0, 1), [mid_keep])]
        (mid_own,), (source_keep,), (source_send,) = combine(
            [
                ([mid_keep, mid_come], 1),
                ([source_sums[0], source_come[0]], 1),
                ([source_sums[2], source_come[1]], 1),
            ],
            [back[0][0]],
        )
        mid_all = exchange(mid_own)
        source_come = swap(source_send, side)
        back.append(attend_back(*self_args, (1, 2), [mid_own]))

        def post(pieces, base, earlier, after):
            flat = [item[0] for item in pieces]
            span = sum(item[0].shape[1] for item in pieces)
            for group in range(len(self_keys)):
                flat += [item[1 + 2 * group] for item in pieces]
                flat += [item[2 + 2 * group] for item in pieces]
            wide = 3 * span + (128 if earlier else 0)
            return run(
                "self_post",
                span // 32,
                functools.partial(
                    self_post_kernel,
                    pieces=len(pieces),
                    base=base,
                    count=row,
                    spans=[item.shape[0] // rows for item in normed_parts],
                    begun=bool(earlier),
                ),
                [*flat, *normed_parts, self_qkv, *earlier],
                [shape(rows, width)] * row
                + [shape(width // 2, wide)] * 2
                + ([] if earlier else [shape(8, span, F32)]),
                after,
                [places],
                [pltpu.VMEM((width, wide), F32)],
            )

        (mid_copies,), (source_grad,) = combine(
            [("copies", mid_all), ([source_keep, source_come], 1)], [back[1][0]]
        )
        mid_half = regather(mid_copies)
        *parts, early_keep, early_send, early_small = post(back, 0, [], [mid_copies])
        early_come = swap(early_send, core)
        last = [attend_back(*self_args, (3, 1), [early_small])]
        *parts, late_keep, late_send = post(
            last, width - 128, [*unit_parts, *parts, early_small], []
        )
        late_come = swap(late_send, core)
        ((late_own,),) = combine([("beside", [early_keep, early_come, late_keep, late_come])])
        return late_own, mid_half, source_grad, grad_first, *parts

    def nothing():
        return jax.tree.map(lambda item: jnp.zeros(item.shape, item.dtype), jax.eval_shape(backward))

    late_own, mid_half, source_grad, grad_first, *parts = lax.cond(
        source_len[0] > 0, backward, nothing
    )
    late_all = exchange(late_own)
    parts_come = [swap(parts[1], core), swap(parts[3], core)]
    cuts = [rows // 4, rows - rows // 4]
    (own_sum,), side_sums = combine(
        [([parts[0], parts_come[0]], 1), ([parts[2], parts_come[1]], cuts)], [late_own]
    )
    own_come = [swap(item, side) for item in side_sums]
    mid_halves = [mid_half, swap(mid_half, core)]
    cross_kv_grad, self_out_grad, cross_q_grad, small_a = place(
        places,
        [
            (
                mid_halves,
                [(width, 2 * width), (width, width), (width, width), (width, 128)],
                [(0, (0, 0), 2 * width), (1, (0, 0), width), (2, (0, 0), width), (3, (0, 0), 128)],
            )
        ],
        [own_sum],
    )
    ffn_in_grad, ffn_out_grad, cross_out_grad = place(
        places,
        [
            (
                [ffn_sums],
                [(width, units), (units, width), (width, width)],
                [(0, (0, 0), units)]
                + [(1, (k * width, 0), width) for k in range(units // width)]
                + [(2, (0, 0), width)],
            )
        ],
        [small_a],
    )
    ((late_copies,),) = combine([("copies", late_all)], [ffn_in_grad, own_come[0]])
    late_half = regather(late_copies)
    (ffn_biases,) = run("biases", 1, biases_kernel, [small_a], [shape(4, width, F32)], [late_copies])
    (tokens_grad,) = run(
        "tokens",
        20,
        tokens_kernel,
        [own_sum, *own_come, grad_first, tokens[0], norm_gain],
        [shape(rows, width)],
        [ffn_biases],
    )
    self_qkv_grad, gains, shifts, projs, outs = run(
        "finish",
        4,
        finish_kernel,
        [late_half, swap(late_half, core), small_a],
        [
            shape(width, 3 * width, F32),
            shape(3, width, F32),
            shape(3, width, F32),
            shape(4, width, F32),
            shape(3, width, F32),
        ],
        [tokens_grad],
        [places],
        [pltpu.VMEM((width, 128), F32)],
    )
    return (
        output[None],
        tokens_grad[None],
        source_grad[None],
        self_qkv_grad,
        self_out_grad,
        cross_q_grad,
        cross_kv_grad,
        cross_out_grad,
        ffn_in_grad,
        ffn_out_grad,
        gains,
        shifts,
        projs,
        outs,
        ffn_biases.reshape(units),
    )


def solution(mesh):
    row_size = mesh.shape["seq"]
    split = jax.sharding.Mesh(
        mesh.devices.reshape(mesh.shape["batch"], row_size // 2, 2), ("batch", "side", "core")
    )
    row = P("batch", ("side", "core"), None)
    flat = P("batch", ("side", "core"))
    return jax.shard_map(
        functools.partial(body, dict(split.shape)),
        mesh=split,
        in_specs=(row, row, row, flat, flat, P("batch")) + (P(),) * 12,
        out_specs=(row, row, row) + (P(),) * 12,
        check_vma=False,
    )
```
